256 devices in a mesh: expert: 64 (over z, x, core), zero: 4 (over y).
Axes of the slice: x: 4, y: 4, z: 8, core: 2. Of those that a mesh axis runs over, the one named last changes fastest.
Arguments:
- cotangent: bfloat16 [32768, 2048], P(('expert', 'zero')), may hold values from -0.59765625 to 0.59765625
- gates: float32 [32768, 8], P(('expert', 'zero')), may hold values from 0.05 to 1
- expert_ids: int32 [32768, 8], P(('expert', 'zero')), may hold values from 0 to 127, all different within a row; in each aligned block of 128 rows (0 to 127, 128 to 255, ...) at most 16 rows name the same one
- hidden: bfloat16 [128, 4096, 768], P('expert', 'zero'), may hold values from -6 to 6
- momentum_left: float32 [128, 768, 32], P('expert', 'zero'), may hold values from -6 to 6
- momentum_right: float32 [128, 32, 2048], P('expert', None, 'zero'), may hold values from -1 to 1
- sketch: float32 [128, 2048, 32], P('expert'), may hold values from -6 to 6
Outputs:
- basis: float32 [128, 768, 32], P('expert', 'zero')
- coefficients: float32 [128, 32, 2048], P('expert', None, 'zero')
The draws below stay inside these ranges and needn't reach their ends.
Inputs may be any that keep to these rules, and one draw needn't show every extreme that they name: `expert_ids`: among the 128 tokens of one device (an aligned block of rows) no expert is named more than 16 times, a bound that some block reaches; the 8 experts of a token differ.
All inputs are finite; a program needn't handle non-finite values.
Results may differ from the reference program's by a relative error of at most 0.0035.
Values may be sent and summed in bfloat16 or wider, within the bound.
No kernel may reach another device: no remote copies, remote signals or barrier semaphores. Data moves between devices by JAX's collectives and lax.ppermute only.
A program may use at most 128 MiB of HBM per device.

```python
import math
import jax
import jax.numpy as jnp
import numpy as np
from jax import lax

D = 2048
FF = 768
TOP = 8
RANK = 32
CAP = 16
TOK_DEV = 128
EXPERTS = 128
TOKENS = 32768
SLOTS = 4096
N_EXPERT = 64
N_ZERO = 4


def steps_of(rng, dims, shards, low, top_value):
    def one(position, blocks):
        draws = jax.random.uniform(jax.random.fold_in(jax.random.fold_in(rng, 6), position), (blocks,), jnp.float32, low / len(shards), top_value / len(shards))
        return jnp.repeat(jnp.exp(draws), dims[position] // blocks).reshape((-1,) + (1,) * (len(dims) - position - 1))

    gain = one(*shards[0])
    for cut in shards[1:]:
        gain = gain * one(*cut)
    return gain


def assign_block(rng, own, number, rows, number_of, top, most, slope):
    sequence = jax.random.permutation(rng, number_of)
    heavy_load, usual = load_shares(number_of, rows * top, most, slope, True), load_shares(number_of, rows * top, most, slope, False)
    places = jnp.arange(number_of)

    def named(tallies, rotation):
        used = int((tallies > 0).sum())
        fixed = max(1, used // 4)
        shifted = fixed + (places - fixed + rotation * (used - fixed)) % max(1, number_of - fixed)
        return jnp.zeros((number_of,), jnp.int32).at[sequence[jnp.where(places < fixed, places, shifted)]].set(jnp.asarray(tallies, jnp.int32))

    tallies = jnp.where(number % 4 == 0, named(heavy_load, number // 4), named(usual, number - number // 4 - 1))
    mixed = jax.random.permutation(jax.random.fold_in(own, 3), number_of)
    giver, receiver = mixed[0:number_of // 2 * 2:2], mixed[1:number_of // 2 * 2:2]
    room = jnp.minimum(tallies[giver] - 1, most - tallies[receiver]) // 2
    room = jnp.where((giver == sequence[0]) | (receiver == sequence[0]) | (tallies[receiver] == 0), 0, jnp.maximum(room, 0))
    shifted = jax.random.randint(jax.random.fold_in(own, 4), (number_of // 2,), 0, 1 << 20) % (room + 1)
    tallies = tallies.at[giver].add(-shifted).at[receiver].add(shifted)
    members = jnp.searchsorted(jnp.cumsum(tallies), jnp.arange(rows * top), side="right").astype(jnp.int32)
    listing = members.reshape(top, rows).T
    listing = listing[jax.random.permutation(jax.random.fold_in(own, 1), rows)]
    rotation = jax.random.randint(jax.random.fold_in(own, 2), (rows, 1), 0, top)
    return jnp.take_along_axis(listing, (jnp.arange(top)[None, :] + rotation) % top, axis=1)


def load_shares(count, total, bound, slope, full):
    loads = [(1 << 20) // math.isqrt(grade ** slope) + 1 for grade in range(1, count + 1)]
    largest = bound if full else min(bound, max(-(-total // count), total * loads[0] // sum(loads)))
    least = 1 if total - largest >= count - 1 else 0
    holding, spare = [largest] + [least] * (count - 1), total - largest - least * (count - 1)
    while spare > 0:
        candidates = [i for i in range(1, count) if holding[i] < largest] or [i for i in range(1, count) if holding[i] < bound]
        whole, remaining = sum([loads[i] for i in candidates]), spare
        for i in candidates:
            more = min(bound - holding[i], max(1, remaining * loads[i] // whole), spare)
            holding[i] = holding[i] + more
            spare = spare - more
    return np.array(holding)


def centred(key, shape, scale, most, split=(), kind=jnp.bfloat16):
    result = jax.random.normal(key, shape, jnp.float32) * scale
    if len(split) > 0:
        result = steps_of(key, shape, split, -0.22, 0.18) * result
    return jnp.clip(result, min=-most, max=most).astype(kind)


def setup_inputs(seed: int = 0) -> dict:
    keys = jax.random.split(jax.random.key(seed), 8)
    cotangent = centred(keys[0], (TOKENS, D), 0.1, 0.59765625, ((0, 256),))
    gates = jnp.clip(jnp.exp(math.log(1.0) - 2.9957323 * jax.random.uniform(keys[1], (TOKENS, TOP), jnp.float32) ** steps_of(keys[1], (TOKENS, TOP), ((0, 256),), -0.2, 0.2)), 0.05, 1.0)
    expert_ids_keys = jax.random.split(jax.random.fold_in(keys[2], 1), TOKENS // TOK_DEV)
    expert_ids_turns = jax.random.permutation(jax.random.fold_in(keys[2], 3), TOKENS // TOK_DEV)
    expert_ids = jax.vmap(lambda own, number: assign_block(jax.random.fold_in(keys[2], 2), own, number, TOK_DEV, EXPERTS, TOP, CAP, 2))(expert_ids_keys, expert_ids_turns).reshape((TOKENS, TOP))
    hidden = centred(keys[3], (EXPERTS, SLOTS, FF), 1.0, 6.0, ((0, 64), (1, 4)))
    momentum_left = centred(keys[4], (EXPERTS, FF, RANK), 1.0, 6.0, ((0, 64), (1, 4)), jnp.float32)
    momentum_right = centred(keys[5], (EXPERTS, RANK, D), RANK ** -0.5, 1.0, ((0, 64), (2, 4)), jnp.float32)
    sketch = centred(keys[6], (EXPERTS, D, RANK), 1.0, 6.0, ((0, 64),), jnp.float32)
    return dict(cotangent=cotangent, gates=gates, expert_ids=expert_ids, hidden=hidden, momentum_left=momentum_left, momentum_right=momentum_right, sketch=sketch)


MOMENTUM_DECAY = 0.9

def slot_table(ids_block, count):
    flat = ids_block.reshape(-1)
    onehot = (flat[:, None] == jnp.arange(count, dtype=jnp.int32)[None, :]).astype(jnp.int32)
    before = jnp.cumsum(onehot, axis=0) - onehot
    return jnp.sum(before * onehot, axis=1).astype(jnp.int32)

def reference(cotangent, gates, expert_ids, hidden, momentum_left, momentum_right, sketch):
    devices = N_EXPERT * N_ZERO
    span = N_EXPERT * CAP
    blocks = expert_ids.reshape(devices, TOK_DEV, TOP)
    slots = jax.vmap(lambda blk: slot_table(blk, EXPERTS))(blocks).reshape(-1)
    flat_ids = expert_ids.reshape(-1).astype(jnp.int32)
    pairs = jnp.arange(TOKENS * TOP, dtype=jnp.int32)
    device = pairs // (TOK_DEV * TOP)
    row = device % N_ZERO * span + device // N_ZERO * CAP + slots
    table = jnp.full((EXPERTS * N_ZERO * span,), -1, jnp.int32)
    table = table.at[flat_ids * (N_ZERO * span) + row].set(pairs).reshape(EXPERTS, N_ZERO * span)
    flat_gates = gates.reshape(-1)
    highest = lax.Precision.HIGHEST

    def per_expert(items):
        held, left, right, test, where = items
        live = where >= 0
        safe = jnp.maximum(where, 0)
        rows = (flat_gates[safe][:, None] * cotangent[safe // TOP].astype(jnp.float32)).astype(jnp.bfloat16)
        rows = jnp.where(live[:, None], rows, jnp.zeros_like(rows))
        grad = jnp.dot(held.T.astype(jnp.float32), rows.astype(jnp.float32), preferred_element_type=jnp.float32)
        merged = MOMENTUM_DECAY * jnp.dot(left, right, precision=highest) + grad
        sketched = jnp.dot(merged, test, precision=highest)
        gram = jnp.dot(sketched.T, sketched, precision=highest) / FF
        lower = jnp.linalg.cholesky(gram)
        basis_t = lax.linalg.triangular_solve(lower, sketched.T, left_side=True, lower=True)
        coeff = jnp.dot(basis_t, merged, precision=highest) / FF
        return (basis_t.T, coeff)
    basis, coefficients = lax.map(per_expert, (hidden, momentum_left, momentum_right, sketch, table))
    return (basis, coefficients)
```

```python
import functools

import jax
import jax.numpy as jnp
from jax import lax
from jax.experimental import pallas as pl
from jax.experimental.pallas import tpu as pltpu
from jax.sharding import PartitionSpec as P

NX, NC = 4, 2
CAP = 16
MOMENTUM_DECAY = 0.9

BF, F32 = jnp.bfloat16, jnp.float32
HIGHEST = lax.Precision.HIGHEST
VMEM = pl.BlockSpec(memory_space=pltpu.VMEM)
SMEM = pl.BlockSpec(memory_space=pltpu.SMEM)
NT = (((1,), (1,)), ((), ()))
NN = (((1,), (0,)), ((), ()))


def dot(a, b, dims=NN, precision=None):
    return lax.dot_general(a, b, dims, precision=precision, preferred_element_type=F32)


def split(v):
    hi = v.astype(BF)
    return hi, (v - hi.astype(F32)).astype(BF)


def stacked(v):
    return jnp.concatenate(split(v), axis=0)


def folded(v):
    half = v.shape[0] // 2
    return v[:half] + v[half:]


def call(kernel, outs, args, specs=None, scratch=(), limit=56 << 20, flops=0):
    return pl.pallas_call(
        kernel,
        out_shape=outs,
        in_specs=specs or [VMEM] * len(args),
        out_specs=jax.tree.map(lambda _: VMEM, outs),
        scratch_shapes=list(scratch),
        compiler_params=pltpu.CompilerParams(vmem_limit_bytes=limit),
        cost_estimate=pl.CostEstimate(flops=flops, bytes_accessed=flops // 500, transcendentals=0),
    )(*args)


def pack_kernel(cot_ref, gates_ref, ids_ref, out_ref):
    tokens, width = cot_ref.shape
    out_ref[:, :width] = cot_ref[...]
    g = gates_ref[...]
    hi = g.astype(BF).astype(F32)
    mid = (g - hi).astype(BF).astype(F32)
    low = g - hi - mid
    ids = ids_ref[...].astype(F32)
    rest = jnp.zeros((tokens - 4 * g.shape[0], tokens), F32)
    out_ref[:, width:] = jnp.concatenate([ids, hi, mid, low, rest], axis=0).astype(BF)


def sketch_kernel(st_ref, out_ref):
    hi, low = split(st_ref[...])
    out_ref[0] = hi
    out_ref[1] = low


def momentum_kernel(meta_ref, st_ref, r_ref, *refs):
    lefts, (full_ref, mom_ref, rows) = refs[:-3], refs[-3:]
    ny, y = len(lefts), meta_ref[0]
    for d in range(ny):
        rows[lax.rem(y - d + ny, ny)] = lefts[d][...]
    local = lefts[0].shape[-1]
    cols = r_ref.shape[-1]
    for i in range(r_ref.shape[0]):
        part = st_ref[i, :, pl.ds(pl.multiple_of(y * cols, 128), cols)]
        inner = dot(part, r_ref[i], NT, HIGHEST) * MOMENTUM_DECAY
        for a in range(ny):
            block = rows[a, i]
            full_ref[i, :, a * local : (a + 1) * local] = block
            mom_ref[i, :, a * local : (a + 1) * local] = dot(inner, block, NN, HIGHEST)


def project_kernel(nb, sizes, meta_ref, *refs):
    pieces, refs = refs[: sum(sizes)], refs[sum(sizes) :]
    sk, (out_ref, pos_ref, gate_ref, all_s, y_scr) = refs[:-5], refs[-5:]
    ng, per = len(sk), sk[0].shape[1]
    count = ng * per // 32
    rows = ng * per
    for d in range(ng):
        all_s[d * per : (d + 1) * per] = sk[d][0]
        all_s[rows + d * per : rows + (d + 1) * per] = sk[d][1]
    blocks, at = [], 0
    for n in sizes:
        blocks.append(pieces[at : at + n])
        at += n
    tokens = sum(p.shape[0] for p in blocks[0])
    width = all_s.shape[1]
    which = lax.broadcasted_iota(jnp.int32, (count, tokens), 0)
    before = (
        lax.broadcasted_iota(jnp.int32, (tokens, tokens), 0)
        < lax.broadcasted_iota(jnp.int32, (tokens, tokens), 1)
    ).astype(F32).astype(BF)
    named, weights = [], []
    for b in range(nb):
        extra = blocks[b][0][0:32, width:].astype(F32)
        ids = extra[0:8]
        g = extra[8:16] + extra[16:24] + extra[24:32]
        member = jnp.zeros((count, tokens), F32)
        gate = jnp.zeros((count, tokens), F32)
        for q in range(count):
            hit = ids == meta_ref[q].astype(F32)
            m = jnp.sum(jnp.where(hit, 1.0, 0.0), axis=0, keepdims=True)
            w = jnp.sum(jnp.where(hit, g, 0.0), axis=0, keepdims=True)
            member = jnp.where(which == q, m, member)
            gate = jnp.where(which == q, w, gate)
        named.append(member)
        weights.append(gate)
    member = jnp.concatenate(named, axis=0)
    slot = dot(member.astype(BF), before)
    for b in range(nb):
        here = slice(b * count, (b + 1) * count)
        base = meta_ref[count + b].astype(F32)
        pos_ref[here] = jnp.where(member[here] > 0.5, slot[here] + base, -1.0)
        gate_ref[here] = weights[b]
    for b in range(0, nb, 2):
        x = jnp.concatenate([p[:, :width] for blk in blocks[b : b + 2] for p in blk], axis=0)
        y_scr[:, b * tokens : b * tokens + x.shape[0]] = folded(dot(all_s[...], x, NT))
    slots = out_ref.shape[-1]
    place = lax.broadcasted_iota(jnp.int32, (slots, nb * tokens), 0).astype(F32)
    for q in range(count):
        line = lambda ref: jnp.concatenate(
            [ref[b * count + q : b * count + q + 1] for b in range(nb)], axis=1
        )
        one = jnp.where(place == line(pos_ref), 1.0, 0.0).astype(BF)
        v = y_scr[q * 32 : (q + 1) * 32] * line(gate_ref)
        out_ref[q] = folded(dot(stacked(v), one, NT))


def sum_kernel(nd, meta_ref, *refs):
    parts, (h_ref, mom_ref, out_ref) = refs[:nd], refs[nd:]
    for i in range(out_ref.shape[0]):
        total = mom_ref[i]
        for d in range(nd):
            h = h_ref[i, :, meta_ref[d]]
            h = h.reshape(-1, h.shape[-1])
            total = total + folded(dot(stacked(parts[d][i]), h))
        out_ref[i] = total


def basis_kernel(ny, nd, meta_ref, *refs):
    parts, (h_ref, basis_ref, z_ref) = refs[:ny], refs[ny:]
    count, rank, ff = basis_ref.shape
    row = lax.broadcasted_iota(jnp.int32, (rank, 2 * rank), 0)
    lane = lax.broadcasted_iota(jnp.int32, (rank, 2 * rank), 1)
    sk, work = [], []
    for i in range(count):
        s = parts[0][i]
        for d in range(1, ny):
            s = s + parts[d][i]
        sk.append(s)
        both = jnp.concatenate([jnp.zeros_like(s), s], axis=0)
        a = dot(s, both, NT, HIGHEST) / ff
        work.append(jnp.where(lane == row, 1.0, a))
    for j in range(rank):
        for i in range(count):
            a = work[i]
            pivot = a[j : j + 1, rank + j : rank + j + 1]
            factor = a[:, rank + j : rank + j + 1] / pivot
            work[i] = a - jnp.where(row > j, factor, 0.0) * a[j : j + 1]
    for i in range(count):
        diag = jnp.sum(jnp.where(lane == row + rank, work[i], 0.0), axis=1, keepdims=True)
        inverse = (work[i] / jnp.sqrt(diag))[:, :rank]
        basis = dot(inverse, sk[i], NN, HIGHEST)
        basis_ref[i] = basis
        b = stacked(basis / ff)
        for d in range(nd):
            h = h_ref[i, :, meta_ref[d]]
            h = h.reshape(-1, h.shape[-1])
            z_ref[d, i] = folded(dot(b, h, NT))


def own_kernel(meta_ref, basis_ref, left_ref, r_ref, out_ref, mom_ref):
    count, rank, ff = basis_ref.shape
    local = out_ref.shape[-1]
    y = meta_ref[0]
    for i in range(count):
        b = basis_ref[i]
        own = b[:, :local]
        for a in range(1, ff // local):
            own = jnp.where(y == a, b[:, a * local : (a + 1) * local], own)
        out_ref[i] = own
        inner = dot(b, left_ref[i], NT, HIGHEST) * (MOMENTUM_DECAY / ff)
        mom_ref[i] = dot(inner, r_ref[i], NN, HIGHEST)


def coefficient_kernel(nb, sizes, nd, *refs):
    pieces, refs = refs[: sum(sizes)], refs[sum(sizes) :]
    zs, (pos_ref, gate_ref, out_ref, w_scr) = refs[:nd], refs[nd:]
    local, rank, slots = zs[0].shape
    count = nd * local
    tokens = pos_ref.shape[1]
    rows = count * rank
    place = lax.broadcasted_iota(jnp.int32, (slots, nb * tokens), 0).astype(F32)
    for q in range(count):
        line = lambda ref: jnp.concatenate(
            [ref[b * count + q : b * count + q + 1] for b in range(nb)], axis=1
        )
        one = jnp.where(place == line(pos_ref), 1.0, 0.0).astype(BF)
        w = folded(dot(stacked(zs[q // local][q % local]), one)) * line(gate_ref)
        hi, low = split(w)
        w_scr[q * rank : (q + 1) * rank] = hi
        w_scr[rows + q * rank : rows + (q + 1) * rank] = low
    step = 256

    @pl.loop(0, out_ref.shape[1] // step)
    def _(n):
        cols = pl.ds(pl.multiple_of(n * step, step), step)
        x = jnp.concatenate([p[:, cols] for p in pieces], axis=0)
        out_ref[:, cols] = folded(dot(w_scr[...], x))


def body(cotangent, gates, expert_ids, hidden, momentum_left, momentum_right, sketch):
    nx, nc = NX, NC
    ne, ny = lax.axis_size("expert"), lax.axis_size("zero")
    nz = ne // (nx * nc)
    local, _, ff = hidden.shape
    tokens, width = cotangent.shape
    rank = sketch.shape[2]
    me, y = lax.axis_index("expert"), lax.axis_index("zero")
    z, x, c = me // (nx * nc), me // nc % nx, me % nc
    ints = lambda *v: jnp.stack([jnp.asarray(n, jnp.int32) for n in v])

    def shift(v, dz=0, dx=0, dc=0):
        pairs = []
        for e in range(ne):
            a, b, k = e // (nx * nc), e // nc % nx, e % nc
            to = ((a + dz) % nz * nx + (b + dx) % nx) * nc + (k + dc) % nc
            pairs.append((e, to))
        return lax.ppermute(v, "expert", pairs)

    def shift_y(v, dy):
        return lax.ppermute(v, "zero", [(a, (a + dy) % ny) for a in range(ny)])

    def shaped(s, t=F32):
        return jax.ShapeDtypeStruct(s, t)

    mine = call(pack_kernel, shaped((tokens, width + tokens), BF), (cotangent, gates.T, expert_ids.T))

    half = nz // 2
    top = tokens // 2
    blocks = [[mine]]
    places = [0]
    right = left = mine
    for k in range(1, half):
        right, left = shift(right, dz=1), shift(left, dz=-1)
        blocks += [[right], [left]]
        places += [k, -k]
    blocks.append([shift(right[:top], dz=1), shift(left[top:], dz=-1)])
    places.append(half)
    others = [[shift(p, dc=1) for p in b] for b in blocks]
    blocks, places = blocks + others, places * 2
    base = [
        lax.rem(z - k + nz, nz) * (nc * CAP) + (c if n < len(places) // 2 else nc - 1 - c) * CAP
        for n, k in enumerate(places)
    ]
    nb = len(blocks)
    sizes = [len(b) for b in blocks]
    pieces = [p for b in blocks for p in b]

    st = jnp.swapaxes(sketch, 1, 2)
    two = call(sketch_kernel, shaped((2, local * rank, width), BF), (st.reshape(local * rank, width),))
    sketches = [two] + [shift(two, dx=-d) for d in range(1, nx)]
    experts = [
        ((z * nx + lax.rem(x + d, nx)) * nc + c) * local + i for d in range(nx) for i in range(local)
    ]

    lt = jnp.swapaxes(momentum_left, 1, 2)
    lefts = [lt] + [shift_y(lt, d) for d in range(1, ny)]
    left_full, mom = call(
        momentum_kernel,
        [shaped((local, rank, ff))] * 2,
        (ints(y), st, momentum_right, *lefts),
        specs=[SMEM] + [VMEM] * (2 + ny),
        scratch=[pltpu.VMEM((ny, local, rank, ff // ny), F32)],
    )

    slots = nz * nc * CAP
    count = nx * local
    products, pos, gate = call(
        functools.partial(project_kernel, nb, sizes),
        [shaped((count, rank, slots)), shaped((nb * count, tokens)), shaped((nb * count, tokens))],
        (ints(*experts, *base), *pieces, *sketches),
        specs=[SMEM] + [VMEM] * (len(pieces) + nx),
        scratch=[
            pltpu.VMEM((2 * count * rank, width), BF),
            pltpu.VMEM((count * rank, nb * tokens), F32),
        ],
        flops=2 * 2 * count * rank * nb * tokens * width,
    )
    products = products.reshape(nx, local, rank, slots)
    products = [products[0]] + [shift(products[d], dx=d) for d in range(1, nx)]

    h = hidden.reshape(local, nz, nx, nc * CAP, ff)
    part = call(
        functools.partial(sum_kernel, nx),
        shaped((local, rank, ff)),
        (ints(*[lax.rem(x - d + nx, nx) for d in range(nx)]), *products, h, mom),
        specs=[SMEM] + [VMEM] * (nx + 2),
    )
    parts = [part] + [shift_y(part, d) for d in range(1, ny)]
    basis, coded = call(
        functools.partial(basis_kernel, ny, nx),
        [shaped((local, rank, ff)), shaped((nx, local, rank, slots))],
        (ints(*[lax.rem(x + d, nx) for d in range(nx)]), *parts, h),
        specs=[SMEM] + [VMEM] * (ny + 1),
    )
    coded = [coded[0]] + [shift(coded[d], dx=d) for d in range(1, nx)]
    coded = [coded[-d % nx] for d in range(nx)]
    own_basis, own_mom = call(
        own_kernel,
        [shaped((local, rank, ff // ny)), shaped(momentum_right.shape)],
        (ints(y), basis, left_full, momentum_right),
        specs=[SMEM] + [VMEM] * 3,
    )
    coeff = call(
        functools.partial(coefficient_kernel, nb, sizes, nx),
        shaped((count * rank, width)),
        (*pieces, *coded, pos, gate),
        scratch=[pltpu.VMEM((2 * count * rank, nb * tokens), BF)],
        flops=2 * 2 * count * rank * nb * tokens * width,
    ).reshape(nx, local, rank, width)
    total = coeff[0]
    for d in range(1, nx):
        total = total + shift(coeff[d], dx=d)
    cols = width // ny

    def columns(d):
        return lax.dynamic_slice_in_dim(total, lax.rem(y + d, ny) * cols, cols, axis=2)

    out = columns(0) + own_mom
    for d in range(1, ny):
        out = out + shift_y(columns(d), d)
    return jnp.swapaxes(own_basis, 1, 2), out


def solution(mesh):
    return jax.shard_map(
        body,
        mesh=mesh,
        in_specs=(
            P(("expert", "zero"), None),
            P(("expert", "zero"), None),
            P(("expert", "zero"), None),
            P("expert", "zero", None),
            P("expert", "zero", None),
            P("expert", None, "zero"),
            P("expert", None, None),
        ),
        out_specs=(P("expert", "zero", None), P("expert", None, "zero")),
        check_vma=False,
    )
```

```python
import functools

import jax
import jax.numpy as jnp
from jax import lax
from jax.experimental import pallas as pl
from jax.experimental.pallas import tpu as pltpu
from jax.sharding import PartitionSpec as P

NX, NC = 4, 2
CAP = 16
MOMENTUM_DECAY = 0.9

BF, F32 = jnp.bfloat16, jnp.float32
HIGHEST = lax.Precision.HIGHEST
VMEM = pl.BlockSpec(memory_space=pltpu.VMEM)
ANY = pl.BlockSpec(memory_space=pl.ANY)
SMEM = pl.BlockSpec(memory_space=pltpu.SMEM)
NT = (((1,), (1,)), ((), ()))
NN = (((1,), (0,)), ((), ()))


def dot(a, b, dims=NN, precision=None):
    return lax.dot_general(a, b, dims, precision=precision, preferred_element_type=F32)


def split(v):
    hi = v.astype(BF)
    return hi, (v - hi.astype(F32)).astype(BF)


def stacked(v):
    return jnp.concatenate(split(v), axis=0)


def folded(v):
    half = v.shape[0] // 2
    return v[:half] + v[half:]


def call(kernel, outs, args, specs=None, scratch=(), limit=30 << 20, flops=0):
    return pl.pallas_call(
        kernel,
        out_shape=outs,
        in_specs=specs or [VMEM] * len(args),
        out_specs=jax.tree.map(lambda _: VMEM, outs),
        scratch_shapes=list(scratch),
        compiler_params=pltpu.CompilerParams(vmem_limit_bytes=limit),
        cost_estimate=pl.CostEstimate(flops=flops, bytes_accessed=flops // 500, transcendentals=0),
    )(*args)


def after(values, *needs):
    return pl.pallas_call(
        lambda *refs: None,
        out_shape=[jax.ShapeDtypeStruct(v.shape, v.dtype) for v in values],
        in_specs=[ANY] * (len(values) + len(needs)),
        out_specs=[ANY] * len(values),
        input_output_aliases={n: n for n in range(len(values))},
    )(*values, *needs)


def pack_kernel(cot_ref, gates_ref, ids_ref, out_ref):
    tokens, width = cot_ref.shape
    out_ref[:, :width] = cot_ref[...]
    g = gates_ref[...]
    hi = g.astype(BF).astype(F32)
    mid = (g - hi).astype(BF).astype(F32)
    low = g - hi - mid
    ids = ids_ref[...].astype(F32)
    rest = jnp.zeros((tokens - 4 * g.shape[0], tokens), F32)
    out_ref[:, width:] = jnp.concatenate([ids, hi, mid, low, rest], axis=0).astype(BF)


def sketch_kernel(st_ref, out_ref):
    hi, low = split(st_ref[...])
    out_ref[0] = hi
    out_ref[1] = low


def momentum_kernel(meta_ref, st_ref, r_ref, *refs):
    lefts, (full_ref, mom_ref, rows) = refs[:-3], refs[-3:]
    ny, y = len(lefts), meta_ref[3]
    for d in range(ny):
        rows[lax.rem(y - d + ny, ny)] = lefts[d][...]
    local = lefts[0].shape[-1]
    cols = r_ref.shape[-1]
    for i in range(r_ref.shape[0]):
        part = st_ref[i, :, pl.ds(pl.multiple_of(y * cols, 128), cols)]
        inner = dot(part, r_ref[i], NT, HIGHEST) * MOMENTUM_DECAY
        for a in range(ny):
            block = rows[a, i]
            full_ref[i, :, a * local : (a + 1) * local] = block
            mom_ref[i, :, a * local : (a + 1) * local] = dot(inner, block, NN, HIGHEST)


def project_kernel(sizes, places, nz, ng, carried, unread, meta_ref, *refs):
    nb = len(sizes)
    pieces, refs = refs[: sum(sizes)], refs[sum(sizes) :]
    sk, refs = refs[:ng], refs[ng:]
    earlier, refs = refs[:carried], refs[carried + unread :]
    outs, (pos_ref, gate_ref, all_s, y_scr) = refs[:ng], refs[ng:]
    per = sk[0].shape[1]
    local = outs[0].shape[0]
    count = ng * local
    rows = ng * per
    for d in range(ng):
        all_s[d * per : (d + 1) * per] = sk[d][0]
        all_s[rows + d * per : rows + (d + 1) * per] = sk[d][1]
    blocks, at = [], 0
    for n in sizes:
        blocks.append(pieces[at : at + n])
        at += n
    tokens = sum(p.shape[0] for p in blocks[0])
    width = all_s.shape[1]
    which = lax.broadcasted_iota(jnp.int32, (count, tokens), 0)
    before = (
        lax.broadcasted_iota(jnp.int32, (tokens, tokens), 0)
        < lax.broadcasted_iota(jnp.int32, (tokens, tokens), 1)
    ).astype(F32).astype(BF)
    z, x, c = meta_ref[0], meta_ref[1], meta_ref[2]
    experts = [
        (((z * NX + lax.rem(x + q // local, ng)) * NC + c) * local + q % local).astype(F32)
        for q in range(count)
    ]
    named, weights = [], []
    for b in range(nb):
        extra = blocks[b][0][0:32, width:].astype(F32)
        ids = extra[0:8]
        g = extra[8:16] + extra[16:24] + extra[24:32]
        member = jnp.zeros((count, tokens), F32)
        gate = jnp.zeros((count, tokens), F32)
        for q in range(count):
            hit = ids == experts[q]
            m = jnp.sum(jnp.where(hit, 1.0, 0.0), axis=0, keepdims=True)
            w = jnp.sum(jnp.where(hit, g, 0.0), axis=0, keepdims=True)
            member = jnp.where(which == q, m, member)
            gate = jnp.where(which == q, w, gate)
        named.append(member)
        weights.append(gate)
    member = jnp.concatenate(named, axis=0)
    slot = dot(member.astype(BF), before)
    for b in range(nb):
        here = slice(b * count, (b + 1) * count)
        source = c if b < len(places) else NC - 1 - c
        base = ((lax.rem(z - places[b % len(places)] + nz, nz) * NC + source) * CAP).astype(F32)
        pos_ref[here] = jnp.where(member[here] > 0.5, slot[here] + base, -1.0)
        gate_ref[here] = weights[b]
    for b in range(0, nb, 2):
        x = jnp.concatenate([p[:, :width] for blk in blocks[b : b + 2] for p in blk], axis=0)
        y_scr[:, b * tokens : b * tokens + x.shape[0]] = folded(dot(all_s[...], x, NT))
    slots = outs[0].shape[-1]
    place = lax.broadcasted_iota(jnp.int32, (slots, nb * tokens), 0).astype(F32)
    for q in range(count):
        line = lambda ref: jnp.concatenate(
            [ref[b * count + q : b * count + q + 1] for b in range(nb)], axis=1
        )
        one = jnp.where(place == line(pos_ref), 1.0, 0.0).astype(BF)
        v = y_scr[q * 32 : (q + 1) * 32] * line(gate_ref)
        r = folded(dot(stacked(v), one, NT))
        outs[q // local][q % local] = r + earlier[q // local][q % local] if carried else r


def sum_kernel(nd, meta_ref, *refs):
    parts, (h_ref, mom_ref, out_ref) = refs[:nd], refs[nd:]
    for i in range(out_ref.shape[0]):
        total = mom_ref[i]
        for d in range(nd):
            h = h_ref[i, :, lax.rem(meta_ref[1] - d + nd, nd)]
            h = h.reshape(-1, h.shape[-1])
            total = total + folded(dot(stacked(parts[d][i]), h))
        out_ref[i] = total


def basis_kernel(ny, nd, meta_ref, *refs):
    parts, (h_ref, basis_ref), zs = refs[:ny], refs[ny : ny + 2], refs[ny + 2 :]
    count, rank, ff = basis_ref.shape
    row = lax.broadcasted_iota(jnp.int32, (rank, 2 * rank), 0)
    lane = lax.broadcasted_iota(jnp.int32, (rank, 2 * rank), 1)
    sk, work = [], []
    for i in range(count):
        s = parts[0][i]
        for d in range(1, ny):
            s = s + parts[d][i]
        sk.append(s)
        both = jnp.concatenate([jnp.zeros_like(s), s], axis=0)
        a = dot(s, both, NT, HIGHEST) / ff
        work.append(jnp.where(lane == row, 1.0, a))
    for j in range(rank):
        for i in range(count):
            a = work[i]
            pivot = a[j : j + 1, rank + j : rank + j + 1]
            factor = a[:, rank + j : rank + j + 1] / pivot
            work[i] = a - jnp.where(row > j, factor, 0.0) * a[j : j + 1]
    for i in range(count):
        diag = jnp.sum(jnp.where(lane == row + rank, work[i], 0.0), axis=1, keepdims=True)
        inverse = (work[i] / jnp.sqrt(diag))[:, :rank]
        basis = dot(inverse, sk[i], NN, HIGHEST)
        basis_ref[i] = basis
        b = stacked(basis / ff)
        for d in range(nd):
            h = h_ref[i, :, lax.rem(meta_ref[1] + d, nd)]
            h = h.reshape(-1, h.shape[-1])
            zs[d][i] = folded(dot(b, h, NT))


def own_kernel(meta_ref, basis_ref, left_ref, r_ref, out_ref, mom_ref):
    count, rank, ff = basis_ref.shape
    local = out_ref.shape[-1]
    y = meta_ref[3]
    for i in range(count):
        b = basis_ref[i]
        own = b[:, :local]
        for a in range(1, ff // local):
            own = jnp.where(y == a, b[:, a * local : (a + 1) * local], own)
        out_ref[i] = own
        inner = dot(b, left_ref[i], NT, HIGHEST) * (MOMENTUM_DECAY / ff)
        mom_ref[i] = dot(inner, r_ref[i], NN, HIGHEST)


def coefficient_kernel(counts, pieces, nd, unread, *refs):
    pieces, refs = refs[:pieces], refs[pieces:]
    zs, refs = refs[:nd], refs[nd:]
    poss, refs = refs[: len(counts)], refs[len(counts) :]
    gates, refs = refs[: len(counts)], refs[len(counts) + unread :]
    outs, w_scr = refs[:nd], refs[nd]
    local, rank, slots = zs[0].shape
    count = nd * local
    nb = sum(counts)
    tokens = poss[0].shape[1]
    rows = count * rank
    place = lax.broadcasted_iota(jnp.int32, (slots, nb * tokens), 0).astype(F32)
    for q in range(count):
        line = lambda group: jnp.concatenate(
            [r[b * count + q : b * count + q + 1] for r, n in zip(group, counts) for b in range(n)],
            axis=1,
        )
        one = jnp.where(place == line(poss), 1.0, 0.0).astype(BF)
        w = folded(dot(stacked(zs[q // local][q % local]), one)) * line(gates)
        hi, low = split(w)
        w_scr[q * rank : (q + 1) * rank] = hi
        w_scr[rows + q * rank : rows + (q + 1) * rank] = low
    step = 256

    @pl.loop(0, outs[0].shape[-1] // step)
    def _(n):
        cols = pl.ds(pl.multiple_of(n * step, step), step)
        x = jnp.concatenate([p[:, cols] for p in pieces], axis=0)
        total = folded(dot(w_scr[...], x))
        for q in range(count):
            ref = outs[q // local]
            ref[q % local, :, cols] = total[q * rank : (q + 1) * rank].astype(ref.dtype)


def body(cotangent, gates, expert_ids, hidden, momentum_left, momentum_right, sketch):
    nx, nc = NX, NC
    ne, ny = lax.axis_size("expert"), lax.axis_size("zero")
    nz = ne // (nx * nc)
    local, _, ff = hidden.shape
    tokens, width = cotangent.shape
    rank = sketch.shape[2]
    me, y = lax.axis_index("expert"), lax.axis_index("zero")
    z, x, c = me // (nx * nc), me // nc % nx, me % nc
    meta = jnp.stack([z, x, c, y]).astype(jnp.int32)

    def shift(v, dz=0, dx=0, dc=0):
        pairs = []
        for e in range(ne):
            a, b, k = e // (nx * nc), e // nc % nx, e % nc
            to = ((a + dz) % nz * nx + (b + dx) % nx) * nc + (k + dc) % nc
            pairs.append((e, to))
        return lax.ppermute(v, "expert", pairs)

    def shift_y(v, dy):
        return lax.ppermute(v, "zero", [(a, (a + dy) % ny) for a in range(ny)])

    def shaped(s, t=F32):
        return jax.ShapeDtypeStruct(s, t)

    mine = call(pack_kernel, shaped((tokens, width + tokens), BF), (cotangent, gates.T, expert_ids.T))

    st = jnp.swapaxes(sketch, 1, 2)
    two = call(sketch_kernel, shaped((2, local * rank, width), BF), (st.reshape(local * rank, width),))
    lt = jnp.swapaxes(momentum_left, 1, 2)
    [mine] = after([mine], two)
    slots = nz * nc * CAP
    count = nx * local

    def project(blocks, places, sketches, earlier, *unread):
        other = [[shift(p, dc=1) for p in b] for b in blocks]
        return functools.partial(project_with, blocks + other, places, sketches, earlier, unread), other

    def project_with(blocks, places, sketches, earlier, unread):
        nb = len(blocks)
        pieces = [p for b in blocks for p in b]
        *products, pos, gate = call(
            functools.partial(
                project_kernel, [len(b) for b in blocks], places, nz, nx, len(earlier), len(unread)
            ),
            [shaped((local, rank, slots))] * nx + [shaped((nb * count, tokens))] * 2,
            (meta, *pieces, *sketches, *earlier, *unread),
            specs=[SMEM] + [VMEM] * (len(pieces) + nx + len(earlier)) + [ANY] * len(unread),
            scratch=[
                pltpu.VMEM((2 * count * rank, width), BF),
                pltpu.VMEM((count * rank, nb * tokens), F32),
            ],
            flops=2 * 2 * count * rank * nb * tokens * width,
        )
        return nb, pieces, products, pos, gate

    half = nz // 2
    top = tokens // 2
    sketches = [two] + [None] * (nx - 1)
    sketches[1], sketches[-1] = shift(two, dx=-1), shift(two, dx=1)
    lefts = [lt] + [shift_y(lt, d) for d in range(1, ny)]
    right, left = shift(mine, dz=1), shift(mine, dz=-1)
    right, left = after([right, left], sketches[1], sketches[-1])
    for d in range(2, nx - 1):
        sketches[d] = shift(two, dx=-d)
    first = [[mine], [right], [left]]
    run, other = project(first, (0, 1, -1), sketches, [])
    left_full, mom = call(
        momentum_kernel,
        [shaped((local, rank, ff))] * 2,
        (meta, st, momentum_right, *lefts),
        specs=[SMEM] + [VMEM] * (2 + ny),
        scratch=[pltpu.VMEM((ny, local, rank, ff // ny), F32)],
    )
    right, left = shift(right, dz=1), shift(left, dz=-1)
    right, left = after([right, left], mom, *sketches[2:-1], *[p for b in other for p in b])
    second = [[right], [left]]
    a = run()
    run, other = project(second, (2, -2), sketches, a[2])
    right, left = shift(right, dz=1), shift(left, dz=-1)
    right, left = after([right, left], a[3], *[p for b in other for p in b])
    third = [[right], [left], [shift(right[:top], dz=1), shift(left[top:], dz=-1)]]
    b = run()
    run, other = project(third, (3, -3, half), sketches, b[2])
    e = run()
    counts = [a[0], b[0], e[0]]
    pieces = a[1] + b[1] + e[1]
    products = [e[2][0]] + [shift(e[2][d], dx=d) for d in range(1, nx)]

    h = hidden.reshape(local, nz, nx, nc * CAP, ff)
    part = call(
        functools.partial(sum_kernel, nx),
        shaped((local, rank, ff)),
        (meta, *products, h, mom),
        specs=[SMEM] + [VMEM] * (nx + 2),
    )
    parts = [part] + [shift_y(part, d) for d in range(1, ny)]
    basis, *coded = call(
        functools.partial(basis_kernel, ny, nx),
        [shaped((local, rank, ff))] + [shaped((local, rank, slots))] * nx,
        (meta, *parts, h),
        specs=[SMEM] + [VMEM] * (ny + 1),
    )
    coded = [coded[0]] + [shift(coded[d], dx=d) for d in range(1, nx)]
    coded = [coded[-d % nx] for d in range(nx)]
    own_basis, own_mom = call(
        own_kernel,
        [shaped((local, rank, ff // ny)), shaped(momentum_right.shape)],
        (meta, basis, left_full, momentum_right),
        specs=[SMEM] + [VMEM] * 3,
    )
    coeff = call(
        functools.partial(coefficient_kernel, counts, len(pieces), nx, 1),
        [shaped((local, rank, width))] + [shaped((local, rank, width), BF)] * (nx - 1),
        (*pieces, *coded, a[3], b[3], e[3], a[4], b[4], e[4], own_mom),
        specs=[VMEM] * (len(pieces) + nx + 6) + [ANY],
        scratch=[pltpu.VMEM((2 * count * rank, sum(counts) * tokens), BF)],
        flops=2 * 2 * count * rank * sum(counts) * tokens * width,
    )
    total = coeff[0]
    for d in range(1, nx):
        total = total + shift(coeff[d], dx=d).astype(F32)
    cols = width // ny

    def columns(d):
        return lax.dynamic_slice_in_dim(total, lax.rem(y + d, ny) * cols, cols, axis=2)

    out = columns(0) + own_mom
    for d in range(1, ny):
        out = out + shift_y(columns(d), d)
    return jnp.swapaxes(own_basis, 1, 2), out


def solution(mesh):
    return jax.shard_map(
        body,
        mesh=mesh,
        in_specs=(
            P(("expert", "zero"), None),
            P(("expert", "zero"), None),
            P(("expert", "zero"), None),
            P("expert", "zero", None),
            P("expert", "zero", None),
            P("expert", None, "zero"),
            P("expert", None, None),
        ),
        out_specs=(P("expert", "zero", None), P("expert", None, "zero")),
        check_vma=False,
    )
```

```python
import functools

import jax
import jax.numpy as jnp
from jax import lax
from jax.experimental import pallas as pl
from jax.experimental.pallas import tpu as pltpu
from jax.sharding import PartitionSpec as P

NX, NC = 4, 2
CAP = 16
MOMENTUM_DECAY = 0.9

BF, F32 = jnp.bfloat16, jnp.float32
HIGHEST = lax.Precision.HIGHEST
VMEM = pl.BlockSpec(memory_space=pltpu.VMEM)
ANY = pl.BlockSpec(memory_space=pl.ANY)
HBM = pl.BlockSpec(memory_space=pltpu.HBM)
SMEM = pl.BlockSpec(memory_space=pltpu.SMEM)
NT = (((1,), (1,)), ((), ()))
NN = (((1,), (0,)), ((), ()))


def dot(a, b, dims=NN, precision=None):
    return lax.dot_general(a, b, dims, precision=precision, preferred_element_type=F32)


def split(v):
    hi = v.astype(BF)
    return hi, (v - hi.astype(F32)).astype(BF)


def stacked(v):
    return jnp.concatenate(split(v), axis=0)


def folded(v):
    half = v.shape[0] // 2
    return v[:half] + v[half:]


def call(kernel, outs, args, specs=None, scratch=(), limit=30 << 20, flops=0):
    return pl.pallas_call(
        kernel,
        out_shape=outs,
        in_specs=specs or [VMEM] * len(args),
        out_specs=jax.tree.map(lambda _: VMEM, outs),
        scratch_shapes=list(scratch),
        compiler_params=pltpu.CompilerParams(vmem_limit_bytes=limit),
        cost_estimate=pl.CostEstimate(flops=flops, bytes_accessed=flops // 500, transcendentals=0),
    )(*args)


def after(values, *needs):
    return pl.pallas_call(
        lambda *refs: None,
        out_shape=[jax.ShapeDtypeStruct(v.shape, v.dtype) for v in values],
        in_specs=[HBM] * len(values) + [ANY] * len(needs),
        out_specs=[HBM] * len(values),
        input_output_aliases={n: n for n in range(len(values))},
    )(*values, *needs)


def pack_kernel(cot_ref, gates_ref, ids_ref, out_ref):
    tokens, width = cot_ref.shape
    out_ref[:, :width] = cot_ref[...]
    g = gates_ref[...]
    hi = g.astype(BF).astype(F32)
    mid = (g - hi).astype(BF).astype(F32)
    low = g - hi - mid
    ids = ids_ref[...].astype(F32)
    rest = jnp.zeros((tokens - 4 * g.shape[0], tokens), F32)
    out_ref[:, width:] = jnp.concatenate([ids, hi, mid, low, rest], axis=0).astype(BF)


def sketch_kernel(st_ref, out_ref):
    hi, low = split(st_ref[...])
    out_ref[0] = hi
    out_ref[1] = low


def momentum_kernel(meta_ref, st_ref, r_ref, *refs):
    lefts, (full_ref, mom_ref, rows) = refs[:-3], refs[-3:]
    ny, y = len(lefts), meta_ref[3]
    for d in range(ny):
        rows[lax.rem(y - d + ny, ny)] = lefts[d][...]
    local = lefts[0].shape[-1]
    cols = r_ref.shape[-1]
    for i in range(r_ref.shape[0]):
        part = st_ref[i, :, pl.ds(pl.multiple_of(y * cols, 128), cols)]
        inner = dot(part, r_ref[i], NT, HIGHEST) * MOMENTUM_DECAY
        for a in range(ny):
            block = rows[a, i]
            full_ref[i, :, a * local : (a + 1) * local] = block
            mom_ref[i, :, a * local : (a + 1) * local] = dot(inner, block, NN, HIGHEST)


def forward_kernel(right_ref, left_ref, hi_ref, low_ref, token_ref):
    hi_ref[...] = right_ref[0]
    low_ref[...] = left_ref[1]
    token_ref[...] = jnp.zeros_like(token_ref)


def gather_kernel(mine_ref, right_ref, left_ref, hi_ref, low_ref, out_ref):
    per = mine_ref.shape[1]
    rows = out_ref.shape[0] // 2
    for d, ref in ((0, mine_ref), (1, right_ref), (3, left_ref)):
        out_ref[d * per : (d + 1) * per] = ref[0]
        out_ref[rows + d * per : rows + (d + 1) * per] = ref[1]
    out_ref[2 * per : 3 * per] = hi_ref[...]
    out_ref[rows + 2 * per : rows + 3 * per] = low_ref[...]


def one_hot(place, line):
    return jnp.where(place == line.astype(BF), jnp.ones((), BF), jnp.zeros((), BF))


def project_kernel(places, nz, ng, carried, meta_ref, *refs):
    nb = len(places)
    pieces, all_s, refs = refs[:nb], refs[nb], refs[nb + 1 :]
    earlier, refs = refs[:carried], refs[carried:]
    outs, (pos_ref, gate_ref, y_scr, x_scr, sems) = refs[:-5], refs[-5:]
    local, rank, slots = outs[0].shape
    count = len(outs) * local
    local = count // ng
    tokens = pieces[0].shape[0]
    width = all_s.shape[1]
    copies = [
        pltpu.make_async_copy(pieces[b], x_scr.at[b * tokens : (b + 1) * tokens], sems.at[b])
        for b in range(nb)
    ]
    for copy in copies:
        copy.start()
    which = lax.broadcasted_iota(jnp.int32, (count, tokens), 0)
    before = (
        lax.broadcasted_iota(jnp.int32, (tokens, tokens), 0)
        < lax.broadcasted_iota(jnp.int32, (tokens, tokens), 1)
    ).astype(F32).astype(BF)
    z, x, c = meta_ref[0], meta_ref[1], meta_ref[2]
    experts = [
        (((z * NX + lax.rem(x + q // local, ng)) * NC + c) * local + q % local).astype(F32)
        for q in range(count)
    ]
    named, weights = [], []
    for b in range(nb):
        copies[b].wait()
        extra = x_scr[b * tokens : b * tokens + 32, width:].astype(F32)
        ids = extra[0:8]
        g = extra[8:16] + extra[16:24] + extra[24:32]
        member = jnp.zeros((count, tokens), F32)
        gate = jnp.zeros((count, tokens), F32)
        for q in range(count):
            hit = ids == experts[q]
            m = jnp.sum(jnp.where(hit, 1.0, 0.0), axis=0, keepdims=True)
            w = jnp.sum(jnp.where(hit, g, 0.0), axis=0, keepdims=True)
            member = jnp.where(which == q, m, member)
            gate = jnp.where(which == q, w, gate)
        named.append(member)
        weights.append(gate)
    member = jnp.concatenate(named, axis=0)
    slot = dot(member.astype(BF), before)
    for b, (k, same) in enumerate(places):
        here = slice(b * count, (b + 1) * count)
        source = c if same else NC - 1 - c
        base = ((lax.rem(z - (1 - 2 * c) * k + nz, nz) * NC + source) * CAP).astype(F32)
        pos_ref[here] = jnp.where(member[here] > 0.5, slot[here] + base, -1.0)
        gate_ref[here] = weights[b]
    for b in range(0, nb, 2):
        pair = slice(b * tokens, (b + 2) * tokens)
        y_scr[:, pair] = folded(dot(all_s[...], x_scr[pair, :width], NT))
    place = lax.broadcasted_iota(jnp.int32, (slots, nb * tokens), 0).astype(F32).astype(BF)
    for q in range(count):
        line = lambda ref: jnp.concatenate(
            [ref[b * count + q : b * count + q + 1] for b in range(nb)], axis=1
        )
        v = y_scr[q * rank : (q + 1) * rank] * line(gate_ref)
        r = folded(dot(stacked(v), one_hot(place, line(pos_ref)), NT))
        per = count // len(outs)
        outs[q // per][q % per] = r + earlier[0][q] if carried else r


def sum_kernel(nd, meta_ref, *refs):
    parts, (h_ref, mom_ref, out_ref) = refs[:nd], refs[nd:]
    for i in range(out_ref.shape[0]):
        total = mom_ref[i]
        for d in range(nd):
            h = h_ref[i, :, lax.rem(meta_ref[1] - d + nd, nd)]
            h = h.reshape(-1, h.shape[-1])
            total = total + folded(dot(stacked(parts[d][i]), h))
        out_ref[i] = total


def basis_kernel(ny, nd, meta_ref, *refs):
    parts, (h_ref, basis_ref), zs = refs[:ny], refs[ny : ny + 2], refs[ny + 2 :]
    count, rank, ff = basis_ref.shape
    row = lax.broadcasted_iota(jnp.int32, (rank, 2 * rank), 0)
    lane = lax.broadcasted_iota(jnp.int32, (rank, 2 * rank), 1)
    sk, work = [], []
    for i in range(count):
        s = parts[0][i]
        for d in range(1, ny):
            s = s + parts[d][i]
        sk.append(s)
        both = jnp.concatenate([jnp.zeros_like(s), s], axis=0)
        a = dot(s, both, NT, HIGHEST) / ff
        work.append(jnp.where(lane == row, 1.0, a))
    for j in range(rank):
        for i in range(count):
            a = work[i]
            pivot = a[j : j + 1, rank + j : rank + j + 1]
            factor = a[:, rank + j : rank + j + 1] / pivot
            work[i] = a - jnp.where(row > j, factor, 0.0) * a[j : j + 1]
    for i in range(count):
        diag = jnp.sum(jnp.where(lane == row + rank, work[i], 0.0), axis=1, keepdims=True)
        inverse = (work[i] / jnp.sqrt(diag))[:, :rank]
        basis = dot(inverse, sk[i], NN, HIGHEST)
        basis_ref[i] = basis
        b = stacked(basis / ff)
        for d in range(nd):
            h = h_ref[i, :, lax.rem(meta_ref[1] + d, nd)]
            h = h.reshape(-1, h.shape[-1])
            zs[d][i] = folded(dot(b, h, NT))


def own_kernel(meta_ref, basis_ref, left_ref, r_ref, out_ref, mom_ref):
    count, rank, ff = basis_ref.shape
    local = out_ref.shape[-1]
    y = meta_ref[3]
    for i in range(count):
        b = basis_ref[i]
        own = b[:, :local]
        for a in range(1, ff // local):
            own = jnp.where(y == a, b[:, a * local : (a + 1) * local], own)
        out_ref[i] = own
        inner = dot(b, left_ref[i], NT, HIGHEST) * (MOMENTUM_DECAY / ff)
        mom_ref[i] = dot(inner, r_ref[i], NN, HIGHEST)


def coefficient_kernel(counts, nd, unread, *refs):
    nb = sum(counts)
    pieces, refs = refs[:nb], refs[nb:]
    zs, refs = refs[:nd], refs[nd:]
    poss, refs = refs[: len(counts)], refs[len(counts) :]
    gates, refs = refs[: len(counts)], refs[len(counts) + unread :]
    outs, (w_scr, x_scr, sems) = refs[:nd], refs[nd:]
    local, rank, slots = zs[0].shape
    count = nd * local
    tokens = poss[0].shape[1]
    rows = count * rank
    width = x_scr.shape[1]
    copies = [
        pltpu.make_async_copy(
            pieces[b].at[:, 0:width], x_scr.at[b * tokens : (b + 1) * tokens], sems.at[b]
        )
        for b in range(nb)
    ]
    for copy in copies:
        copy.start()
    place = lax.broadcasted_iota(jnp.int32, (slots, nb * tokens), 0).astype(F32).astype(BF)
    for q in range(count):
        line = lambda group: jnp.concatenate(
            [r[b * count + q : b * count + q + 1] for r, n in zip(group, counts) for b in range(n)],
            axis=1,
        )
        w = folded(dot(stacked(zs[q // local][q % local]), one_hot(place, line(poss)))) * line(gates)
        hi, low = split(w)
        w_scr[q * rank : (q + 1) * rank] = hi
        w_scr[rows + q * rank : rows + (q + 1) * rank] = low
    for copy in copies:
        copy.wait()
    step = 256

    @pl.loop(0, width // step)
    def _(n):
        cols = pl.ds(pl.multiple_of(n * step, step), step)
        total = folded(dot(w_scr[...], x_scr[:, cols]))
        for q in range(count):
            ref = outs[q // local]
            ref[q % local, :, cols] = total[q * rank : (q + 1) * rank].astype(ref.dtype)


def body(cotangent, gates, expert_ids, hidden, momentum_left, momentum_right, sketch):
    nx, nc = NX, NC
    ne, ny = lax.axis_size("expert"), lax.axis_size("zero")
    nz = ne // (nx * nc)
    local, _, ff = hidden.shape
    tokens, width = cotangent.shape
    rank = sketch.shape[2]
    me, y = lax.axis_index("expert"), lax.axis_index("zero")
    z, x, c = me // (nx * nc), me // nc % nx, me % nc
    meta = jnp.stack([z, x, c, y]).astype(jnp.int32)

    def shift(v, dz=0, dx=0, dc=0):
        pairs = []
        for e in range(ne):
            a, b, k = e // (nx * nc), e // nc % nx, e % nc
            to = ((a + dz) % nz * nx + (b + dx) % nx) * nc + (k + dc) % nc
            pairs.append((e, to))
        return lax.ppermute(v, "expert", pairs)

    def shift_y(v, dy):
        return lax.ppermute(v, "zero", [(a, (a + dy) % ny) for a in range(ny)])

    def shaped(s, t=F32):
        return jax.ShapeDtypeStruct(s, t)

    mine = call(pack_kernel, shaped((tokens, width + tokens), BF), (cotangent, gates.T, expert_ids.T))

    st = jnp.swapaxes(sketch, 1, 2)
    rows = local * rank
    two = call(sketch_kernel, shaped((2, rows, width), BF), (st.reshape(rows, width),))
    lt = jnp.swapaxes(momentum_left, 1, 2)
    slots = nz * nc * CAP
    count = nx * local
    half = nz // 2

    def along(v):
        pairs = []
        for e in range(ne):
            a, b, k = e // (nx * nc), e // nc % nx, e % nc
            pairs.append((e, ((a + 1 - 2 * k) % nz * nx + b) * nc + k))
        return lax.ppermute(v, "expert", pairs)

    def swap(v):
        return shift(v, dc=1)

    def project(named, earlier, parts=1):
        places, blocks = zip(*named)
        nb = len(blocks)
        *products, pos, gate = call(
            functools.partial(project_kernel, places, nz, nx, len(earlier)),
            [shaped((count // parts, rank, slots))] * parts + [shaped((nb * count, tokens))] * 2,
            (meta, *blocks, all_s, *earlier),
            specs=[SMEM] + [ANY] * nb + [VMEM] * (1 + len(earlier)),
            scratch=[
                pltpu.VMEM((count * rank, nb * tokens), F32),
                pltpu.VMEM((nb * tokens, width + tokens), BF),
                pltpu.SemaphoreType.DMA((nb,)),
            ],
            flops=2 * 2 * count * rank * nb * tokens * width,
        )
        return nb, blocks, products, pos, gate

    def ring(k, p, q):
        return [((k, 1), p), ((k, 0), q), ((-k, 0), swap(p)), ((-k, 1), swap(q))]

    p = along(mine)
    sibling = swap(mine)
    q = along(sibling)
    near = [shift(two, dx=-1), shift(two, dx=1)]
    first = [((0, 1), mine), ((0, 0), sibling)] + ring(1, p, q)
    hi, low, token = call(
        forward_kernel, [shaped((rows, width), BF)] * 2 + [shaped((8, 128))], near
    )
    far = [shift(hi, dx=-1), shift(low, dx=1)]
    p, q = after([along(p), along(q)], token)
    second = ring(2, p, q)
    all_s = call(gather_kernel, shaped((2 * count * rank, width), BF), (two, *near, *far))
    a = project(first, [])
    p, q = after([along(p), along(q)], a[3])
    third = ring(3, p, q)
    b = project(second, a[2])
    [p] = after([along(p)], b[3])
    third += [((4, 1), p), ((4, 0), swap(p))]
    e = project(third, b[2], nx)
    lefts = [lt] + [shift_y(lt, d) for d in range(1, ny)]
    left_full, mom = call(
        momentum_kernel,
        [shaped((local, rank, ff))] * 2,
        (meta, st, momentum_right, *lefts),
        specs=[SMEM] + [VMEM] * (2 + ny),
        scratch=[pltpu.VMEM((ny, local, rank, ff // ny), F32)],
    )
    counts = [a[0], b[0], e[0]]
    pieces = a[1] + b[1] + e[1]
    products = [e[2][0]] + [shift(e[2][d], dx=d) for d in range(1, nx)]

    h = hidden.reshape(local, nz, nx, nc * CAP, ff)
    part = call(
        functools.partial(sum_kernel, nx),
        shaped((local, rank, ff)),
        (meta, *products, h, mom),
        specs=[SMEM] + [VMEM] * (nx + 2),
    )
    parts = [part] + [shift_y(part, d) for d in range(1, ny)]
    basis, *coded = call(
        functools.partial(basis_kernel, ny, nx),
        [shaped((local, rank, ff))] + [shaped((local, rank, slots))] * nx,
        (meta, *parts, h),
        specs=[SMEM] + [VMEM] * (ny + 1),
    )
    coded = [coded[0]] + [shift(coded[d], dx=d) for d in range(1, nx)]
    coded = [coded[-d % nx] for d in range(nx)]
    own_basis, own_mom = call(
        own_kernel,
        [shaped((local, rank, ff // ny)), shaped(momentum_right.shape)],
        (meta, basis, left_full, momentum_right),
        specs=[SMEM] + [VMEM] * 3,
    )
    coeff = call(
        functools.partial(coefficient_kernel, counts, nx, 1),
        [shaped((local, rank, width))] + [shaped((local, rank, width), BF)] * (nx - 1),
        (*pieces, *coded, a[3], b[3], e[3], a[4], b[4], e[4], own_mom),
        specs=[ANY] * len(pieces) + [VMEM] * (nx + 6) + [ANY],
        scratch=[
            pltpu.VMEM((2 * count * rank, sum(counts) * tokens), BF),
            pltpu.VMEM((sum(counts) * tokens, width), BF),
            pltpu.SemaphoreType.DMA((len(pieces),)),
        ],
        flops=2 * 2 * count * rank * sum(counts) * tokens * width,
    )
    total = coeff[0]
    for d in range(1, nx):
        total = total + shift(coeff[d], dx=d).astype(F32)
    cols = width // ny

    def columns(d):
        return lax.dynamic_slice_in_dim(total, lax.rem(y + d, ny) * cols, cols, axis=2)

    out = columns(0) + own_mom
    for d in range(1, ny):
        out = out + shift_y(columns(d), d)
    return jnp.swapaxes(own_basis, 1, 2), out


def solution(mesh):
    return jax.shard_map(
        body,
        mesh=mesh,
        in_specs=(
            P(("expert", "zero"), None),
            P(("expert", "zero"), None),
            P(("expert", "zero"), None),
            P("expert", "zero", None),
            P("expert", "zero", None),
            P("expert", None, "zero"),
            P("expert", None, None),
        ),
        out_specs=(P("expert", "zero", None), P("expert", None, "zero")),
        check_vma=False,
    )
```

```python
import functools

import jax
import jax.numpy as jnp
from jax import lax
from jax.experimental import pallas as pl
from jax.experimental.pallas import tpu as pltpu
from jax.sharding import PartitionSpec as P

NX, NC = 4, 2
CAP = 16
MOMENTUM_DECAY = 0.9

WIDE, NARROW = 20 << 20, 12 << 20

BF, F32 = jnp.bfloat16, jnp.float32
HIGHEST = lax.Precision.HIGHEST
VMEM = pl.BlockSpec(memory_space=pltpu.VMEM)
ANY = pl.BlockSpec(memory_space=pl.ANY)
HBM = pl.BlockSpec(memory_space=pltpu.HBM)
SMEM = pl.BlockSpec(memory_space=pltpu.SMEM)
NT = (((1,), (1,)), ((), ()))
NN = (((1,), (0,)), ((), ()))


def dot(a, b, dims=NN, precision=None):
    return lax.dot_general(a, b, dims, precision=precision, preferred_element_type=F32)


def split(v):
    hi = v.astype(BF)
    return hi, (v - hi.astype(F32)).astype(BF)


def stacked(v):
    return jnp.concatenate(split(v), axis=0)


def folded(v):
    half = v.shape[0] // 2
    return v[:half] + v[half:]


def call(kernel, outs, args, specs=None, scratch=(), limit=WIDE, flops=0, spaces=None):
    return pl.pallas_call(
        kernel,
        out_shape=outs,
        in_specs=specs or [VMEM] * len(args),
        out_specs=spaces or jax.tree.map(lambda _: VMEM, outs),
        scratch_shapes=list(scratch),
        compiler_params=pltpu.CompilerParams(vmem_limit_bytes=limit),
        cost_estimate=pl.CostEstimate(flops=flops, bytes_accessed=flops // 500, transcendentals=0),
    )(*args)


def after(values, *needs):
    def kernel(*refs):
        for n in range(len(values)):
            refs[len(values) + len(needs) + n][...] = refs[n][...]

    outs = [jax.ShapeDtypeStruct(v.shape, v.dtype) for v in values]
    return call(kernel, outs, (*values, *needs), limit=NARROW)


def pack_kernel(cot_ref, gates_ref, ids_ref, out_ref, g_scr, i_scr, e_scr, sems):
    tokens, width = cot_ref.shape
    main = pltpu.make_async_copy(cot_ref, out_ref.at[:, 0:width], sems.at[0])
    first = pltpu.make_async_copy(gates_ref, g_scr, sems.at[1])
    second = pltpu.make_async_copy(ids_ref, i_scr, sems.at[2])
    main.start()
    first.start()
    second.start()
    first.wait()
    second.wait()
    g = g_scr[...]
    hi = g.astype(BF).astype(F32)
    mid = (g - hi).astype(BF).astype(F32)
    low = g - hi - mid
    ids = i_scr[...].astype(F32)
    rest = jnp.zeros((tokens - 4 * g.shape[0], tokens), F32)
    e_scr[...] = jnp.concatenate([ids, hi, mid, low, rest], axis=0).astype(BF)
    last = pltpu.make_async_copy(e_scr, out_ref.at[:, width : width + tokens], sems.at[3])
    last.start()
    main.wait()
    last.wait()


def sketch_kernel(st_ref, out_ref):
    hi, low = split(st_ref[...])
    out_ref[0] = hi
    out_ref[1] = low


def momentum_kernel(meta_ref, st_ref, r_ref, *refs):
    lefts, (full_ref, mom_ref, rows) = refs[:-3], refs[-3:]
    ny, y = len(lefts), meta_ref[3]
    for d in range(ny):
        rows[lax.rem(y - d + ny, ny)] = lefts[d][...]
    local = lefts[0].shape[-1]
    cols = r_ref.shape[-1]
    for i in range(r_ref.shape[0]):
        part = st_ref[i, :, pl.ds(pl.multiple_of(y * cols, 128), cols)]
        inner = dot(part, r_ref[i], NT, HIGHEST) * MOMENTUM_DECAY
        for a in range(ny):
            block = rows[a, i]
            full_ref[i, :, a * local : (a + 1) * local] = block
            mom_ref[i, :, a * local : (a + 1) * local] = dot(inner, block, NN, HIGHEST)


def forward_kernel(meta_ref, right_ref, left_ref, out_ref, token_ref):
    out_ref[...] = jnp.where(meta_ref[2] == 0, right_ref[...], left_ref[...])
    token_ref[...] = jnp.zeros_like(token_ref)


def one_hot(place, line):
    return jnp.where(place == line.astype(BF), jnp.ones((), BF), jnp.zeros((), BF))


def project_kernel(places, nz, ng, carried, whole, meta_ref, *refs):
    nb = len(places)
    pieces, refs = refs[:nb], refs[nb:]
    fed = 1 if whole else ng
    sketches, earlier, refs = refs[:fed], refs[fed : fed + carried], refs[fed + carried :]
    outs, (pos_ref, y_scr) = refs[:-2], refs[-2:]
    all_s = sketches[0] if whole else outs[-1]
    outs = outs if whole else outs[:-1]
    _, rank, slots = outs[0].shape
    count = len(outs) * outs[0].shape[0]
    local = count // ng
    rows = count * rank
    gates = nb * count
    tokens = pieces[0].shape[0]
    width = all_s.shape[1]
    if not whole:
        per = rows // ng
        for d in range(ng):
            for k in range(2):
                at = k * rows + d * per
                all_s[at : at + per] = sketches[d][k]
    which = lax.broadcasted_iota(jnp.int32, (count, tokens), 0)
    before = (
        lax.broadcasted_iota(jnp.int32, (tokens, tokens), 0)
        < lax.broadcasted_iota(jnp.int32, (tokens, tokens), 1)
    ).astype(F32).astype(BF)
    z, x, c = meta_ref[0], meta_ref[1], meta_ref[2]
    experts = [
        (((z * NX + lax.rem(x + q // local, ng)) * NC + c) * local + q % local).astype(F32)
        for q in range(count)
    ]
    named, weights = [], []
    for b in range(nb):
        extra = pieces[b][0:32, width:].astype(F32)
        ids = extra[0:8]
        g = extra[8:16] + extra[16:24] + extra[24:32]
        member = jnp.zeros((count, tokens), F32)
        gate = jnp.zeros((count, tokens), F32)
        for q in range(count):
            hit = ids == experts[q]
            m = jnp.sum(jnp.where(hit, 1.0, 0.0), axis=0, keepdims=True)
            w = jnp.sum(jnp.where(hit, g, 0.0), axis=0, keepdims=True)
            member = jnp.where(which == q, m, member)
            gate = jnp.where(which == q, w, gate)
        named.append(member)
        weights.append(gate)
    member = jnp.concatenate(named, axis=0)
    slot = dot(member.astype(BF), before)
    for b, (k, same) in enumerate(places):
        here = slice(b * count, (b + 1) * count)
        source = c if same else NC - 1 - c
        base = ((lax.rem(z - (1 - 2 * c) * k + nz, nz) * NC + source) * CAP).astype(F32)
        pos_ref[here] = jnp.where(member[here] > 0.5, slot[here] + base, -1.0)
        pos_ref[gates + b * count : gates + (b + 1) * count] = weights[b]
    for b in range(0, nb, 2):
        pair = slice(b * tokens, (b + 2) * tokens)
        x2 = jnp.concatenate([ref[:, :width] for ref in pieces[b : b + 2]], axis=0)
        y_scr[:, pair] = folded(dot(all_s[...], x2, NT))
    place = lax.broadcasted_iota(jnp.int32, (slots, nb * tokens), 0).astype(F32).astype(BF)
    for q in range(count):
        line = lambda at: jnp.concatenate(
            [pos_ref[at + b * count + q : at + b * count + q + 1] for b in range(nb)], axis=1
        )
        v = y_scr[q * rank : (q + 1) * rank] * line(gates)
        r = folded(dot(stacked(v), one_hot(place, line(0)), NT))
        per = count // len(outs)
        outs[q // per][q % per] = r + earlier[0][q] if carried else r


def sum_kernel(nd, meta_ref, *refs):
    parts, (h_ref, mom_ref, out_ref) = refs[:nd], refs[nd:]
    for i in range(out_ref.shape[0]):
        total = mom_ref[i]
        for d in range(nd):
            h = h_ref[i, :, lax.rem(meta_ref[1] - d + nd, nd)]
            h = h.reshape(-1, h.shape[-1])
            total = total + folded(dot(stacked(parts[d][i]), h))
        out_ref[i] = total


def basis_kernel(ny, nd, meta_ref, *refs):
    parts, (h_ref, basis_ref), zs = refs[:ny], refs[ny : ny + 2], refs[ny + 2 :]
    count, rank, ff = basis_ref.shape
    row = lax.broadcasted_iota(jnp.int32, (rank, 2 * rank), 0)
    lane = lax.broadcasted_iota(jnp.int32, (rank, 2 * rank), 1)
    sk, work = [], []
    for i in range(count):
        s = parts[0][i]
        for d in range(1, ny):
            s = s + parts[d][i]
        sk.append(s)
        both = jnp.concatenate([jnp.zeros_like(s), s], axis=0)
        a = dot(s, both, NT, HIGHEST) / ff
        work.append(jnp.where(lane == row, 1.0, a))
    for j in range(rank):
        for i in range(count):
            a = work[i]
            pivot = a[j : j + 1, rank + j : rank + j + 1]
            factor = a[:, rank + j : rank + j + 1] / pivot
            work[i] = a - jnp.where(row > j, factor, 0.0) * a[j : j + 1]
    for i in range(count):
        diag = jnp.sum(jnp.where(lane == row + rank, work[i], 0.0), axis=1, keepdims=True)
        inverse = (work[i] / jnp.sqrt(diag))[:, :rank]
        basis = dot(inverse, sk[i], NN, HIGHEST)
        basis_ref[i] = basis
        b = stacked(basis / ff)
        for d in range(nd):
            h = h_ref[i, :, lax.rem(meta_ref[1] + d, nd)]
            h = h.reshape(-1, h.shape[-1])
            zs[d][i] = folded(dot(b, h, NT))


def own_kernel(meta_ref, basis_ref, left_ref, r_ref, out_ref, mom_ref):
    count, rank, ff = basis_ref.shape
    local = out_ref.shape[-1]
    y = meta_ref[3]
    for i in range(count):
        b = basis_ref[i]
        own = b[:, :local]
        for a in range(1, ff // local):
            own = jnp.where(y == a, b[:, a * local : (a + 1) * local], own)
        out_ref[i] = own
        inner = dot(b, left_ref[i], NT, HIGHEST) * (MOMENTUM_DECAY / ff)
        mom_ref[i] = dot(inner, r_ref[i], NN, HIGHEST)


def coefficient_kernel(counts, nd, unread, *refs):
    nb = sum(counts)
    pieces, refs = refs[:nb], refs[nb:]
    zs, refs = refs[:nd], refs[nd:]
    poss, refs = refs[: len(counts)], refs[len(counts) + unread :]
    outs, w_scr = refs[:nd], refs[nd]
    local, rank, slots = zs[0].shape
    count = nd * local
    tokens = poss[0].shape[1]
    rows = count * rank
    width = outs[0].shape[-1]
    place = lax.broadcasted_iota(jnp.int32, (slots, nb * tokens), 0).astype(F32).astype(BF)
    for q in range(count):
        line = lambda gate: jnp.concatenate(
            [
                r[(gate * n + b) * count + q : (gate * n + b) * count + q + 1]
                for r, n in zip(poss, counts)
                for b in range(n)
            ],
            axis=1,
        )
        w = folded(dot(stacked(zs[q // local][q % local]), one_hot(place, line(0)))) * line(1)
        hi, low = split(w)
        w_scr[q * rank : (q + 1) * rank] = hi
        w_scr[rows + q * rank : rows + (q + 1) * rank] = low
    step = 256

    @pl.loop(0, width // step)
    def _(n):
        cols = pl.ds(pl.multiple_of(n * step, step), step)
        x = jnp.concatenate([ref[:, cols] for ref in pieces], axis=0)
        total = folded(dot(w_scr[...], x))
        for q in range(count):
            ref = outs[q // local]
            ref[q % local, :, cols] = total[q * rank : (q + 1) * rank].astype(ref.dtype)


def body(cotangent, gates, expert_ids, hidden, momentum_left, momentum_right, sketch):
    nx, nc = NX, NC
    ne, ny = lax.axis_size("expert"), lax.axis_size("zero")
    nz = ne // (nx * nc)
    local, _, ff = hidden.shape
    tokens, width = cotangent.shape
    rank = sketch.shape[2]
    me, y = lax.axis_index("expert"), lax.axis_index("zero")
    z, x, c = me // (nx * nc), me // nc % nx, me % nc
    meta = jnp.stack([z, x, c, y]).astype(jnp.int32)

    def shift(v, dz=0, dx=0, dc=0):
        pairs = []
        for e in range(ne):
            a, b, k = e // (nx * nc), e // nc % nx, e % nc
            to = ((a + dz) % nz * nx + (b + dx) % nx) * nc + (k + dc) % nc
            pairs.append((e, to))
        return lax.ppermute(v, "expert", pairs)

    def shift_y(v, dy):
        return lax.ppermute(v, "zero", [(a, (a + dy) % ny) for a in range(ny)])

    def shaped(s, t=F32):
        return jax.ShapeDtypeStruct(s, t)

    mine = call(
        pack_kernel,
        shaped((tokens, width + tokens), BF),
        (cotangent, gates.T, expert_ids.T),
        specs=[ANY] * 3,
        scratch=[
            pltpu.VMEM((gates.shape[1], tokens), F32),
            pltpu.VMEM((gates.shape[1], tokens), jnp.int32),
            pltpu.VMEM((tokens, tokens), BF),
            pltpu.SemaphoreType.DMA((4,)),
        ],
    )

    st = jnp.swapaxes(sketch, 1, 2)
    rows = local * rank
    two = call(sketch_kernel, shaped((2, rows, width), BF), (st.reshape(rows, width),))
    lt = jnp.swapaxes(momentum_left, 1, 2)
    slots = nz * nc * CAP
    count = nx * local
    half = nz // 2

    def along(v, axis="z"):
        pairs = []
        for e in range(ne):
            a, b, k = e // (nx * nc), e // nc % nx, e % nc
            if axis == "z":
                pairs.append((e, ((a + 1 - 2 * k) % nz * nx + b) * nc + k))
            else:
                pairs.append((e, (a * nx + (b - 1 + 2 * k) % nx) * nc + k))
        return lax.ppermute(v, "expert", pairs)

    def swap(v):
        return shift(v, dc=1)

    def project(named, sketches, earlier, parts=1):
        places, blocks = zip(*named)
        nb = len(blocks)
        whole = len(sketches) == 1
        outs = [shaped((count // parts, rank, slots))] * parts
        products = call(
            functools.partial(project_kernel, places, nz, nx, len(earlier), whole),
            outs
            + ([] if whole else [shaped((2 * count * rank, width), BF)])
            + [shaped((2 * nb * count, tokens))],
            (meta, *blocks, *sketches, *earlier),
            specs=[SMEM] + [VMEM] * (nb + len(sketches) + len(earlier)),
            scratch=[pltpu.VMEM((count * rank, nb * tokens), F32)],
            flops=2 * 2 * count * rank * nb * tokens * width,
        )
        return nb, blocks, products[:parts], products[-1], products[-2]

    def ring(k, p, q):
        return [((k, 1), p), ((k, 0), q), ((-k, 0), swap(p)), ((-k, 1), swap(q))]

    p = along(mine)
    sibling = swap(mine)
    q = along(sibling)
    near = [shift(two, dx=-1), shift(two, dx=1)]
    first = [((0, 1), mine), ((0, 0), sibling)] + ring(1, p, q)
    farther, token = call(
        forward_kernel,
        [shaped((2, rows, width), BF), shaped((8, 128))],
        (meta, *near),
        specs=[SMEM, VMEM, VMEM],
    )
    far = along(farther, "x")
    lefts = [lt] + [shift_y(lt, d) for d in range(1, ny)]
    left_full, mom = call(
        momentum_kernel,
        [shaped((local, rank, ff))] * 2,
        (meta, st, momentum_right, *lefts),
        specs=[SMEM] + [VMEM] * (2 + ny),
        scratch=[pltpu.VMEM((ny, local, rank, ff // ny), F32)],
    )
    p, q = after([along(p), along(q)], token)
    second = ring(2, p, q)
    a = project(first, [two, near[0], far, near[1]], [])
    all_s = [a[4]]
    p, q = after([along(p), along(q)], a[3], mom)
    third = ring(3, p, q)
    b = project(second, all_s, a[2])
    [p] = after([along(p)], b[3])
    fourth = [((4, 1), p), ((4, 0), swap(p))]
    e = project(third, all_s, b[2])
    f = project(fourth, all_s, e[2], nx)
    steps = [a, b, e, f]
    counts = [v[0] for v in steps]
    pieces = [block for v in steps for block in v[1]]
    products = [f[2][0]] + [shift(f[2][d], dx=d) for d in range(1, nx)]

    h = hidden.reshape(local, nz, nx, nc * CAP, ff)
    part = call(
        functools.partial(sum_kernel, nx),
        shaped((local, rank, ff)),
        (meta, *products, h, mom),
        specs=[SMEM] + [VMEM] * (nx + 2),
        limit=NARROW,
    )
    parts = [part] + [shift_y(part, d) for d in range(1, ny)]
    basis, *coded = call(
        functools.partial(basis_kernel, ny, nx),
        [shaped((local, rank, ff))] + [shaped((local, rank, slots))] * nx,
        (meta, *parts, h),
        specs=[SMEM] + [VMEM] * (ny + 1),
        limit=NARROW,
    )
    coded = [coded[0]] + [shift(coded[d], dx=d) for d in range(1, nx)]
    coded = [coded[-d % nx] for d in range(nx)]
    own_basis, own_mom = call(
        own_kernel,
        [shaped((local, rank, ff // ny)), shaped(momentum_right.shape)],
        (meta, basis, left_full, momentum_right),
        specs=[SMEM] + [VMEM] * 3,
        limit=NARROW,
    )
    coeff = call(
        functools.partial(coefficient_kernel, counts, nx, 1),
        [shaped((local, rank, width))] + [shaped((local, rank, width), BF)] * (nx - 1),
        (*pieces, *coded, *[v[3] for v in steps], own_mom),
        specs=[VMEM] * (len(pieces) + nx + len(steps) + 1),
        limit=WIDE,
        scratch=[
            pltpu.VMEM((2 * count * rank, sum(counts) * tokens), BF),
        ],
        flops=2 * 2 * count * rank * sum(counts) * tokens * width,
    )
    total = coeff[0]
    for d in range(1, nx):
        total = total + shift(coeff[d], dx=d).astype(F32)
    cols = width // ny

    def columns(d):
        return lax.dynamic_slice_in_dim(total, lax.rem(y + d, ny) * cols, cols, axis=2)

    out = columns(0) + own_mom
    for d in range(1, ny):
        out = out + shift_y(columns(d), d)
    return jnp.swapaxes(own_basis, 1, 2), out


def solution(mesh):
    return jax.shard_map(
        body,
        mesh=mesh,
        in_specs=(
            P(("expert", "zero"), None),
            P(("expert", "zero"), None),
            P(("expert", "zero"), None),
            P("expert", "zero", None),
            P("expert", "zero", None),
            P("expert", None, "zero"),
            P("expert", None, None),
        ),
        out_specs=(P("expert", "zero", None), P("expert", None, "zero")),
        check_vma=False,
    )
```

```python
import functools

import jax
import jax.numpy as jnp
from jax import lax
from jax.experimental import pallas as pl
from jax.experimental.pallas import tpu as pltpu
from jax.sharding import PartitionSpec as P

NX, NC = 4, 2
CAP = 16
MOMENTUM_DECAY = 0.9

WIDE, NARROW = 20 << 20, 8 << 20

BF, F32 = jnp.bfloat16, jnp.float32
HIGHEST = lax.Precision.HIGHEST
VMEM = pl.BlockSpec(memory_space=pltpu.VMEM)
ANY = pl.BlockSpec(memory_space=pl.ANY)
HBM = pl.BlockSpec(memory_space=pltpu.HBM)
SMEM = pl.BlockSpec(memory_space=pltpu.SMEM)
NT = (((1,), (1,)), ((), ()))
NN = (((1,), (0,)), ((), ()))


def dot(a, b, dims=NN, precision=None):
    return lax.dot_general(a, b, dims, precision=precision, preferred_element_type=F32)


def split(v):
    hi = v.astype(BF)
    return hi, (v - hi.astype(F32)).astype(BF)


def stacked(v):
    return jnp.concatenate(split(v), axis=0)


def folded(v):
    half = v.shape[0] // 2
    return v[:half] + v[half:]


def call(kernel, outs, args, specs=None, scratch=(), limit=WIDE, flops=0, spaces=None):
    return pl.pallas_call(
        kernel,
        out_shape=outs,
        in_specs=specs or [VMEM] * len(args),
        out_specs=spaces or jax.tree.map(lambda _: VMEM, outs),
        scratch_shapes=list(scratch),
        compiler_params=pltpu.CompilerParams(vmem_limit_bytes=limit),
        cost_estimate=pl.CostEstimate(flops=flops, bytes_accessed=flops // 500, transcendentals=0),
    )(*args)


def after(values, *needs):
    def kernel(*refs):
        for n in range(len(values)):
            refs[len(values) + len(needs) + n][...] = refs[n][...]

    outs = [jax.ShapeDtypeStruct(v.shape, v.dtype) for v in values]
    return call(kernel, outs, (*values, *needs), limit=NARROW)


def pack_kernel(cot_ref, gates_ref, ids_ref, out_ref, g_scr, i_scr, e_scr, sems):
    tokens, width = cot_ref.shape
    main = pltpu.make_async_copy(cot_ref, out_ref.at[:, 0:width], sems.at[0])
    first = pltpu.make_async_copy(gates_ref, g_scr, sems.at[1])
    second = pltpu.make_async_copy(ids_ref, i_scr, sems.at[2])
    main.start()
    first.start()
    second.start()
    first.wait()
    second.wait()
    g = g_scr[...]
    hi = g.astype(BF).astype(F32)
    mid = (g - hi).astype(BF).astype(F32)
    low = g - hi - mid
    ids = i_scr[...].astype(F32)
    rest = jnp.zeros((tokens - 4 * g.shape[0], tokens), F32)
    e_scr[...] = jnp.concatenate([ids, hi, mid, low, rest], axis=0).astype(BF)
    last = pltpu.make_async_copy(e_scr, out_ref.at[:, width : width + tokens], sems.at[3])
    last.start()
    main.wait()
    last.wait()


def sketch_kernel(st_ref, out_ref):
    hi, low = split(st_ref[...])
    out_ref[0] = hi
    out_ref[1] = low


def momentum_kernel(meta_ref, st_ref, r_ref, *refs):
    lefts, (full_ref, mom_ref, rows) = refs[:-3], refs[-3:]
    ny, y = len(lefts), meta_ref[3]
    for d in range(ny):
        rows[lax.rem(y - d + ny, ny)] = lefts[d][...]
    local = lefts[0].shape[-1]
    cols = r_ref.shape[-1]
    for i in range(r_ref.shape[0]):
        part = st_ref[i, :, pl.ds(pl.multiple_of(y * cols, 128), cols)]
        inner = dot(part, r_ref[i], NT, HIGHEST) * MOMENTUM_DECAY
        for a in range(ny):
            block = rows[a, i]
            full_ref[i, :, a * local : (a + 1) * local] = block
            mom_ref[i, :, a * local : (a + 1) * local] = dot(inner, block, NN, HIGHEST)


def forward_kernel(meta_ref, right_ref, left_ref, out_ref, token_ref):
    out_ref[...] = jnp.where(meta_ref[2] == 0, right_ref[...], left_ref[...])
    token_ref[...] = jnp.zeros_like(token_ref)


def one_hot(place, line):
    return jnp.where(place == line.astype(BF), jnp.ones((), BF), jnp.zeros((), BF))


def project_kernel(places, nz, ng, carried, whole, meta_ref, *refs):
    nb = len(places)
    pieces, refs = refs[:nb], refs[nb:]
    fed = 1 if whole else ng
    sketches, earlier, refs = refs[:fed], refs[fed : fed + carried], refs[fed + carried :]
    outs, (pos_ref, y_scr) = refs[:-2], refs[-2:]
    all_s = sketches[0] if whole else outs[-1]
    outs = outs if whole else outs[:-1]
    _, rank, slots = outs[0].shape
    count = len(outs) * outs[0].shape[0]
    local = count // ng
    rows = count * rank
    gates = nb * count
    tokens = pieces[0].shape[0]
    width = all_s.shape[1]
    if not whole:
        per = rows // ng
        for d in range(ng):
            for k in range(2):
                at = k * rows + d * per
                all_s[at : at + per] = sketches[d][k]
    which = lax.broadcasted_iota(jnp.int32, (count, tokens), 0)
    before = (
        lax.broadcasted_iota(jnp.int32, (tokens, tokens), 0)
        < lax.broadcasted_iota(jnp.int32, (tokens, tokens), 1)
    ).astype(F32).astype(BF)
    z, x, c = meta_ref[0], meta_ref[1], meta_ref[2]
    experts = [
        (((z * NX + lax.rem(x + q // local, ng)) * NC + c) * local + q % local).astype(F32)
        for q in range(count)
    ]
    named, weights = [], []
    for b in range(nb):
        extra = pieces[b][0:32, width:].astype(F32)
        ids = extra[0:8]
        g = extra[8:16] + extra[16:24] + extra[24:32]
        member = jnp.zeros((count, tokens), F32)
        gate = jnp.zeros((count, tokens), F32)
        for q in range(count):
            hit = ids == experts[q]
            m = jnp.sum(jnp.where(hit, 1.0, 0.0), axis=0, keepdims=True)
            w = jnp.sum(jnp.where(hit, g, 0.0), axis=0, keepdims=True)
            member = jnp.where(which == q, m, member)
            gate = jnp.where(which == q, w, gate)
        named.append(member)
        weights.append(gate)
    member = jnp.concatenate(named, axis=0)
    slot = dot(member.astype(BF), before)
    for b, (k, same) in enumerate(places):
        here = slice(b * count, (b + 1) * count)
        source = c if same else NC - 1 - c
        base = ((lax.rem(z - (1 - 2 * c) * k + nz, nz) * NC + source) * CAP).astype(F32)
        pos_ref[here] = jnp.where(member[here] > 0.5, slot[here] + base, -1.0)
        pos_ref[gates + b * count : gates + (b + 1) * count] = weights[b]
    for b in range(0, nb, 2):
        pair = slice(b * tokens, (b + 2) * tokens)
        x2 = jnp.concatenate([ref[:, :width] for ref in pieces[b : b + 2]], axis=0)
        y_scr[:, pair] = folded(dot(all_s[...], x2, NT))
    place = lax.broadcasted_iota(jnp.int32, (slots, nb * tokens), 0).astype(F32).astype(BF)
    for q in range(count):
        line = lambda at: jnp.concatenate(
            [pos_ref[at + b * count + q : at + b * count + q + 1] for b in range(nb)], axis=1
        )
        v = y_scr[q * rank : (q + 1) * rank] * line(gates)
        r = folded(dot(stacked(v), one_hot(place, line(0)), NT))
        per = count // len(outs)
        outs[q // per][q % per] = r + earlier[0][q] if carried else r


def sum_kernel(nd, meta_ref, *refs):
    parts, (h_ref, mom_ref, out_ref) = refs[:nd], refs[nd:]
    for i in range(out_ref.shape[0]):
        total = mom_ref[i]
        for d in range(nd):
            h = h_ref[i, :, lax.rem(meta_ref[1] - d + nd, nd)]
            h = h.reshape(-1, h.shape[-1])
            total = total + folded(dot(stacked(parts[d][i]), h))
        out_ref[i] = total


def basis_kernel(ny, nd, meta_ref, *refs):
    parts, (h_ref, basis_ref), zs = refs[:ny], refs[ny : ny + 2], refs[ny + 2 :]
    count, rank, ff = basis_ref.shape
    row = lax.broadcasted_iota(jnp.int32, (rank, 2 * rank), 0)
    lane = lax.broadcasted_iota(jnp.int32, (rank, 2 * rank), 1)
    sk, work = [], []
    for i in range(count):
        s = parts[0][i]
        for d in range(1, ny):
            s = s + parts[d][i]
        sk.append(s)
        both = jnp.concatenate([jnp.zeros_like(s), s], axis=0)
        a = dot(s, both, NT, HIGHEST) / ff
        work.append(jnp.where(lane == row, 1.0, a))
    for j in range(rank):
        for i in range(count):
            a = work[i]
            pivot = a[j : j + 1, rank + j : rank + j + 1]
            factor = a[:, rank + j : rank + j + 1] / pivot
            work[i] = a - jnp.where(row > j, factor, 0.0) * a[j : j + 1]
    for i in range(count):
        diag = jnp.sum(jnp.where(lane == row + rank, work[i], 0.0), axis=1, keepdims=True)
        inverse = (work[i] / jnp.sqrt(diag))[:, :rank]
        basis = dot(inverse, sk[i], NN, HIGHEST)
        basis_ref[i] = basis
        b = stacked(basis / ff)
        for d in range(nd):
            h = h_ref[i, :, lax.rem(meta_ref[1] + d, nd)]
            h = h.reshape(-1, h.shape[-1])
            zs[d][i] = folded(dot(b, h, NT))


def own_kernel(meta_ref, basis_ref, left_ref, r_ref, out_ref, mom_ref):
    count, rank, ff = basis_ref.shape
    local = out_ref.shape[-1]
    y = meta_ref[3]
    for i in range(count):
        b = basis_ref[i]
        own = b[:, :local]
        for a in range(1, ff // local):
            own = jnp.where(y == a, b[:, a * local : (a + 1) * local], own)
        out_ref[i] = own
        inner = dot(b, left_ref[i], NT, HIGHEST) * (MOMENTUM_DECAY / ff)
        mom_ref[i] = dot(inner, r_ref[i], NN, HIGHEST)


def coefficient_kernel(counts, skipped, nd, unread, *refs):
    nb = sum(counts)
    pieces, refs = refs[:nb], refs[nb:]
    zs, refs = refs[:nd], refs[nd:]
    poss, refs = refs[: len(counts)], refs[len(counts) + unread :]
    outs, w_scr = refs[:nd], refs[nd]
    local, rank, slots = zs[0].shape
    count = nd * local
    every = poss[0].shape[0] // (2 * counts[0])
    tokens = poss[0].shape[1]
    rows = count * rank
    width = outs[0].shape[-1]
    place = lax.broadcasted_iota(jnp.int32, (slots, nb * tokens), 0).astype(F32).astype(BF)
    for q in range(count):
        line = lambda gate: jnp.concatenate(
            [
                r[(gate * n + b) * every + skipped + q : (gate * n + b) * every + skipped + q + 1]
                for r, n in zip(poss, counts)
                for b in range(n)
            ],
            axis=1,
        )
        w = folded(dot(stacked(zs[q // local][q % local]), one_hot(place, line(0)))) * line(1)
        hi, low = split(w)
        w_scr[q * rank : (q + 1) * rank] = hi
        w_scr[rows + q * rank : rows + (q + 1) * rank] = low
    step = 256

    @pl.loop(0, width // step)
    def _(n):
        cols = pl.ds(pl.multiple_of(n * step, step), step)
        x = jnp.concatenate([ref[:, cols] for ref in pieces], axis=0)
        total = folded(dot(w_scr[...], x))
        for q in range(count):
            ref = outs[q // local]
            ref[q % local, :, cols] = total[q * rank : (q + 1) * rank].astype(ref.dtype)


def body(cotangent, gates, expert_ids, hidden, momentum_left, momentum_right, sketch):
    nx, nc = NX, NC
    ne, ny = lax.axis_size("expert"), lax.axis_size("zero")
    nz = ne // (nx * nc)
    local, _, ff = hidden.shape
    tokens, width = cotangent.shape
    rank = sketch.shape[2]
    me, y = lax.axis_index("expert"), lax.axis_index("zero")
    z, x, c = me // (nx * nc), me // nc % nx, me % nc
    meta = jnp.stack([z, x, c, y]).astype(jnp.int32)

    def shift(v, dz=0, dx=0, dc=0):
        pairs = []
        for e in range(ne):
            a, b, k = e // (nx * nc), e // nc % nx, e % nc
            to = ((a + dz) % nz * nx + (b + dx) % nx) * nc + (k + dc) % nc
            pairs.append((e, to))
        return lax.ppermute(v, "expert", pairs)

    def shift_y(v, dy):
        return lax.ppermute(v, "zero", [(a, (a + dy) % ny) for a in range(ny)])

    def shaped(s, t=F32):
        return jax.ShapeDtypeStruct(s, t)

    mine = call(
        pack_kernel,
        shaped((tokens, width + tokens), BF),
        (cotangent, gates.T, expert_ids.T),
        specs=[ANY] * 3,
        limit=58 << 20,
        scratch=[
            pltpu.VMEM((gates.shape[1], tokens), F32),
            pltpu.VMEM((gates.shape[1], tokens), jnp.int32),
            pltpu.VMEM((tokens, tokens), BF),
            pltpu.SemaphoreType.DMA((4,)),
        ],
    )

    st = jnp.swapaxes(sketch, 1, 2)
    rows = local * rank
    two = call(sketch_kernel, shaped((2, rows, width), BF), (st.reshape(rows, width),))
    lt = jnp.swapaxes(momentum_left, 1, 2)
    slots = nz * nc * CAP
    count = nx * local
    half = nz // 2

    def along(v, axis="z"):
        pairs = []
        for e in range(ne):
            a, b, k = e // (nx * nc), e // nc % nx, e % nc
            if axis == "z":
                pairs.append((e, ((a + 1 - 2 * k) % nz * nx + b) * nc + k))
            else:
                pairs.append((e, (a * nx + (b - 1 + 2 * k) % nx) * nc + k))
        return lax.ppermute(v, "expert", pairs)

    def swap(v):
        return shift(v, dc=1)

    def project(named, sketches, earlier, parts=1):
        places, blocks = zip(*named)
        nb = len(blocks)
        whole = len(sketches) == 1
        outs = [shaped((count // parts, rank, slots))] * parts
        products = call(
            functools.partial(project_kernel, places, nz, nx, len(earlier), whole),
            outs
            + ([] if whole else [shaped((2 * count * rank, width), BF)])
            + [shaped((2 * nb * count, tokens))],
            (meta, *blocks, *sketches, *earlier),
            specs=[SMEM] + [VMEM] * (nb + len(sketches) + len(earlier)),
            scratch=[pltpu.VMEM((count * rank, nb * tokens), F32)],
            flops=2 * 2 * count * rank * nb * tokens * width,
        )
        return nb, blocks, products[:parts], products[-1], products[-2]

    def ring(k, p, q):
        return [((k, 1), p), ((k, 0), q), ((-k, 0), swap(p)), ((-k, 1), swap(q))]

    p = along(mine)
    sibling = swap(mine)
    q = along(sibling)
    near = [shift(two, dx=-1), shift(two, dx=1)]
    first = [((0, 1), mine), ((0, 0), sibling)] + ring(1, p, q)
    farther, token = call(
        forward_kernel,
        [shaped((2, rows, width), BF), shaped((8, 128))],
        (meta, *near),
        specs=[SMEM, VMEM, VMEM],
    )
    far = along(farther, "x")
    lefts = [lt] + [shift_y(lt, d) for d in range(1, ny)]
    left_full, mom = call(
        momentum_kernel,
        [shaped((local, rank, ff))] * 2,
        (meta, st, momentum_right, *lefts),
        specs=[SMEM] + [VMEM] * (2 + ny),
        scratch=[pltpu.VMEM((ny, local, rank, ff // ny), F32)],
    )
    [p], q = after([along(p)], token, mom), along(q)
    second = ring(2, p, q)
    a = project(first, [two, near[0], far, near[1]], [])
    all_s = [a[4]]
    [p], q = after([along(p)], a[3]), along(q)
    third = ring(3, p, q)
    b = project(second, all_s, a[2])
    [p] = after([along(p)], b[3])
    fourth = [((4, 1), p), ((4, 0), swap(p))]
    e = project(third, all_s, b[2])
    f = project(fourth, all_s, e[2], nx)
    steps = [a, b, e, f]
    counts = [v[0] for v in steps]
    pieces = [block for v in steps for block in v[1]]
    products = [f[2][0]] + [shift(f[2][d], dx=d) for d in range(1, nx)]

    h = hidden.reshape(local, nz, nx, nc * CAP, ff)
    part = call(
        functools.partial(sum_kernel, nx),
        shaped((local, rank, ff)),
        (meta, *products, h, mom),
        specs=[SMEM] + [VMEM] * (nx + 2),
        limit=NARROW,
    )
    parts = [part] + [shift_y(part, d) for d in range(1, ny)]
    basis, *coded = call(
        functools.partial(basis_kernel, ny, nx),
        [shaped((local, rank, ff))] + [shaped((local, rank, slots))] * nx,
        (meta, *parts, h),
        specs=[SMEM] + [VMEM] * (ny + 1),
        limit=NARROW,
    )
    coded = [coded[0]] + [shift(coded[d], dx=d) for d in range(1, nx)]
    coded = [coded[-d % nx] for d in range(nx)]
    own_basis, own_mom = call(
        own_kernel,
        [shaped((local, rank, ff // ny)), shaped(momentum_right.shape)],
        (meta, basis, left_full, momentum_right),
        specs=[SMEM] + [VMEM] * 3,
        limit=NARROW,
    )
    def coefficients(groups, *unread):
        return call(
            functools.partial(
                coefficient_kernel, counts, groups[0] * local, len(groups), len(unread)
            ),
            [shaped((local, rank, width), BF if d else F32) for d in groups],
            (*pieces, *[coded[d] for d in groups], *[v[3] for v in steps], *unread),
            scratch=[pltpu.VMEM((2 * len(groups) * local * rank, sum(counts) * tokens), BF)],
            flops=2 * 2 * len(groups) * local * rank * sum(counts) * tokens * width,
        )

    coeff = coefficients(list(range(nx)), own_mom)
    total = coeff[0]
    for d in range(1, nx):
        total = total + shift(coeff[d], dx=d).astype(F32)
    cols = width // ny

    def columns(d):
        return lax.dynamic_slice_in_dim(total, lax.rem(y + d, ny) * cols, cols, axis=2)

    out = columns(0) + own_mom
    for d in range(1, ny):
        out = out + shift_y(columns(d), d)
    return jnp.swapaxes(own_basis, 1, 2), out


def solution(mesh):
    return jax.shard_map(
        body,
        mesh=mesh,
        in_specs=(
            P(("expert", "zero"), None),
            P(("expert", "zero"), None),
            P(("expert", "zero"), None),
            P("expert", "zero", None),
            P("expert", "zero", None),
            P("expert", None, "zero"),
            P("expert", None, None),
        ),
        out_specs=(P("expert", "zero", None), P("expert", None, "zero")),
        check_vma=False,
    )
```

```python
import functools

import jax
import jax.numpy as jnp
from jax import lax
from jax.experimental import pallas as pl
from jax.experimental.pallas import tpu as pltpu
from jax.sharding import PartitionSpec as P

NX, NC = 4, 2
CAP = 16
MOMENTUM_DECAY = 0.9

WIDE, NARROW = 20 << 20, 8 << 20

BF, F32 = jnp.bfloat16, jnp.float32
HIGHEST = lax.Precision.HIGHEST
VMEM = pl.BlockSpec(memory_space=pltpu.VMEM)
ANY = pl.BlockSpec(memory_space=pl.ANY)
HBM = pl.BlockSpec(memory_space=pltpu.HBM)
SMEM = pl.BlockSpec(memory_space=pltpu.SMEM)
NT = (((1,), (1,)), ((), ()))
NN = (((1,), (0,)), ((), ()))


def dot(a, b, dims=NN, precision=None):
    return lax.dot_general(a, b, dims, precision=precision, preferred_element_type=F32)


def split(v):
    hi = v.astype(BF)
    return hi, (v - hi.astype(F32)).astype(BF)


def stacked(v):
    return jnp.concatenate(split(v), axis=0)


def folded(v):
    half = v.shape[0] // 2
    return v[:half] + v[half:]


def call(kernel, outs, args, specs=None, scratch=(), limit=WIDE, flops=0, spaces=None):
    return pl.pallas_call(
        kernel,
        out_shape=outs,
        in_specs=specs or [VMEM] * len(args),
        out_specs=spaces or jax.tree.map(lambda _: VMEM, outs),
        scratch_shapes=list(scratch),
        compiler_params=pltpu.CompilerParams(vmem_limit_bytes=limit),
        cost_estimate=pl.CostEstimate(flops=flops, bytes_accessed=flops // 500, transcendentals=0),
    )(*args)


def after(values, *needs):
    def kernel(*refs):
        for n in range(len(values)):
            refs[len(values) + len(needs) + n][...] = refs[n][...]

    outs = [jax.ShapeDtypeStruct(v.shape, v.dtype) for v in values]
    return call(kernel, outs, (*values, *needs), limit=NARROW)


def pack_kernel(cot_ref, gates_ref, ids_ref, out_ref, g_scr, i_scr, e_scr, sems):
    tokens, width = cot_ref.shape
    main = pltpu.make_async_copy(cot_ref, out_ref.at[:, 0:width], sems.at[0])
    first = pltpu.make_async_copy(gates_ref, g_scr, sems.at[1])
    second = pltpu.make_async_copy(ids_ref, i_scr, sems.at[2])
    main.start()
    first.start()
    second.start()
    first.wait()
    second.wait()
    g = g_scr[...]
    hi = g.astype(BF).astype(F32)
    mid = (g - hi).astype(BF).astype(F32)
    low = g - hi - mid
    ids = i_scr[...].astype(F32)
    rest = jnp.zeros((tokens - 4 * g.shape[0], tokens), F32)
    e_scr[...] = jnp.concatenate([ids, hi, mid, low, rest], axis=0).astype(BF)
    last = pltpu.make_async_copy(e_scr, out_ref.at[:, width : width + tokens], sems.at[3])
    last.start()
    main.wait()
    last.wait()


def sketch_kernel(st_ref, out_ref):
    hi, low = split(st_ref[...])
    out_ref[0] = hi
    out_ref[1] = low


def momentum_kernel(meta_ref, st_ref, r_ref, *refs):
    lefts, (full_ref, mom_ref, rows) = refs[:-3], refs[-3:]
    ny, y = len(lefts), meta_ref[3]
    for d in range(ny):
        rows[lax.rem(y - d + ny, ny)] = lefts[d][...]
    local = lefts[0].shape[-1]
    cols = r_ref.shape[-1]
    for i in range(r_ref.shape[0]):
        part = st_ref[i, :, pl.ds(pl.multiple_of(y * cols, 128), cols)]
        inner = dot(part, r_ref[i], NT, HIGHEST) * MOMENTUM_DECAY
        for a in range(ny):
            block = rows[a, i]
            full_ref[i, :, a * local : (a + 1) * local] = block
            mom_ref[i, :, a * local : (a + 1) * local] = dot(inner, block, NN, HIGHEST)


def forward_kernel(meta_ref, right_ref, left_ref, out_ref, token_ref):
    out_ref[...] = jnp.where(meta_ref[2] == 0, right_ref[...], left_ref[...])
    token_ref[...] = jnp.zeros_like(token_ref)


def one_hot(place, line):
    return jnp.where(place == line.astype(BF), jnp.ones((), BF), jnp.zeros((), BF))


def project_kernel(places, nz, ng, carried, whole, meta_ref, *refs):
    nb = len(places)
    pieces, refs = refs[:nb], refs[nb:]
    fed = 1 if whole else ng
    sketches, earlier, refs = refs[:fed], refs[fed : fed + carried], refs[fed + carried :]
    outs, (pos_ref, y_scr) = refs[:-2], refs[-2:]
    all_s = sketches[0] if whole else outs[-1]
    outs = outs if whole else outs[:-1]
    _, rank, slots = outs[0].shape
    count = len(outs) * outs[0].shape[0]
    local = count // ng
    rows = count * rank
    gates = nb * count
    tokens = pieces[0].shape[0]
    width = all_s.shape[1]
    if not whole:
        per = rows // ng
        for d in range(ng):
            for k in range(2):
                at = k * rows + d * per
                all_s[at : at + per] = sketches[d][k]
    which = lax.broadcasted_iota(jnp.int32, (count, tokens), 0)
    before = (
        lax.broadcasted_iota(jnp.int32, (tokens, tokens), 0)
        < lax.broadcasted_iota(jnp.int32, (tokens, tokens), 1)
    ).astype(F32).astype(BF)
    z, x, c = meta_ref[0], meta_ref[1], meta_ref[2]
    experts = [
        (((z * NX + lax.rem(x + q // local, ng)) * NC + c) * local + q % local).astype(F32)
        for q in range(count)
    ]
    named, weights = [], []
    for b in range(nb):
        extra = pieces[b][0:32, width:].astype(F32)
        ids = extra[0:8]
        g = extra[8:16] + extra[16:24] + extra[24:32]
        member = jnp.zeros((count, tokens), F32)
        gate = jnp.zeros((count, tokens), F32)
        for q in range(count):
            hit = ids == experts[q]
            m = jnp.sum(jnp.where(hit, 1.0, 0.0), axis=0, keepdims=True)
            w = jnp.sum(jnp.where(hit, g, 0.0), axis=0, keepdims=True)
            member = jnp.where(which == q, m, member)
            gate = jnp.where(which == q, w, gate)
        named.append(member)
        weights.append(gate)
    member = jnp.concatenate(named, axis=0)
    slot = dot(member.astype(BF), before)
    for b, (k, same) in enumerate(places):
        here = slice(b * count, (b + 1) * count)
        source = c if same else NC - 1 - c
        base = ((lax.rem(z - (1 - 2 * c) * k + nz, nz) * NC + source) * CAP).astype(F32)
        pos_ref[here] = jnp.where(member[here] > 0.5, slot[here] + base, -1.0)
        pos_ref[gates + b * count : gates + (b + 1) * count] = weights[b]
    for b in range(0, nb, 2):
        pair = slice(b * tokens, (b + 2) * tokens)
        x2 = jnp.concatenate([ref[:, :width] for ref in pieces[b : b + 2]], axis=0)
        y_scr[:, pair] = folded(dot(all_s[...], x2, NT))
    place = lax.broadcasted_iota(jnp.int32, (slots, nb * tokens), 0).astype(F32).astype(BF)
    for q in range(count):
        line = lambda at: jnp.concatenate(
            [pos_ref[at + b * count + q : at + b * count + q + 1] for b in range(nb)], axis=1
        )
        v = y_scr[q * rank : (q + 1) * rank] * line(gates)
        r = folded(dot(stacked(v), one_hot(place, line(0)), NT))
        per = count // len(outs)
        outs[q // per][q % per] = r + earlier[0][q] if carried else r


def sum_kernel(nd, meta_ref, *refs):
    parts, (h_ref, mom_ref, out_ref) = refs[:nd], refs[nd:]
    for i in range(out_ref.shape[0]):
        total = mom_ref[i]
        for d in range(nd):
            h = h_ref[i, :, lax.rem(meta_ref[1] - d + nd, nd)]
            h = h.reshape(-1, h.shape[-1])
            total = total + folded(dot(stacked(parts[d][i]), h))
        out_ref[i] = total


def basis_kernel(ny, nd, meta_ref, *refs):
    parts, (h_ref, basis_ref), zs = refs[:ny], refs[ny : ny + 2], refs[ny + 2 :]
    count, rank, ff = basis_ref.shape
    row = lax.broadcasted_iota(jnp.int32, (rank, 2 * rank), 0)
    lane = lax.broadcasted_iota(jnp.int32, (rank, 2 * rank), 1)
    sk, work = [], []
    for i in range(count):
        s = parts[0][i]
        for d in range(1, ny):
            s = s + parts[d][i]
        sk.append(s)
        both = jnp.concatenate([jnp.zeros_like(s), s], axis=0)
        a = dot(s, both, NT, HIGHEST) / ff
        work.append(jnp.where(lane == row, 1.0, a))
    for j in range(rank):
        for i in range(count):
            a = work[i]
            pivot = a[j : j + 1, rank + j : rank + j + 1]
            factor = a[:, rank + j : rank + j + 1] / pivot
            work[i] = a - jnp.where(row > j, factor, 0.0) * a[j : j + 1]
    for i in range(count):
        diag = jnp.sum(jnp.where(lane == row + rank, work[i], 0.0), axis=1, keepdims=True)
        inverse = (work[i] / jnp.sqrt(diag))[:, :rank]
        basis = dot(inverse, sk[i], NN, HIGHEST)
        basis_ref[i] = basis
        b = stacked(basis / ff)
        for d in range(nd):
            h = h_ref[i, :, lax.rem(meta_ref[1] + d, nd)]
            h = h.reshape(-1, h.shape[-1])
            zs[d][i] = folded(dot(b, h, NT))


def own_kernel(meta_ref, basis_ref, left_ref, r_ref, out_ref, mom_ref):
    count, rank, ff = basis_ref.shape
    local = out_ref.shape[-1]
    y = meta_ref[3]
    for i in range(count):
        b = basis_ref[i]
        own = b[:, :local]
        for a in range(1, ff // local):
            own = jnp.where(y == a, b[:, a * local : (a + 1) * local], own)
        out_ref[i] = own
        inner = dot(b, left_ref[i], NT, HIGHEST) * (MOMENTUM_DECAY / ff)
        mom_ref[i] = dot(inner, r_ref[i], NN, HIGHEST)


def coefficient_kernel(counts, skipped, nd, unread, *refs):
    nb = sum(counts)
    pieces, refs = refs[:nb], refs[nb:]
    zs, refs = refs[:nd], refs[nd:]
    poss, refs = refs[: len(counts)], refs[len(counts) + unread :]
    outs, w_scr = refs[:nd], refs[nd]
    local, rank, slots = zs[0].shape
    count = nd * local
    every = poss[0].shape[0] // (2 * counts[0])
    tokens = poss[0].shape[1]
    rows = count * rank
    width = outs[0].shape[-1]
    place = lax.broadcasted_iota(jnp.int32, (slots, nb * tokens), 0).astype(F32).astype(BF)
    for q in range(count):
        line = lambda gate: jnp.concatenate(
            [
                r[(gate * n + b) * every + skipped + q : (gate * n + b) * every + skipped + q + 1]
                for r, n in zip(poss, counts)
                for b in range(n)
            ],
            axis=1,
        )
        w = folded(dot(stacked(zs[q // local][q % local]), one_hot(place, line(0)))) * line(1)
        hi, low = split(w)
        w_scr[q * rank : (q + 1) * rank] = hi
        w_scr[rows + q * rank : rows + (q + 1) * rank] = low
    step = 256

    @pl.loop(0, width // step)
    def _(n):
        cols = pl.ds(pl.multiple_of(n * step, step), step)
        x = jnp.concatenate([ref[:, cols] for ref in pieces], axis=0)
        total = folded(dot(w_scr[...], x))
        for q in range(count):
            ref = outs[q // local]
            ref[q % local, :, cols] = total[q * rank : (q + 1) * rank].astype(ref.dtype)


def body(cotangent, gates, expert_ids, hidden, momentum_left, momentum_right, sketch):
    nx, nc = NX, NC
    ne, ny = lax.axis_size("expert"), lax.axis_size("zero")
    nz = ne // (nx * nc)
    local, _, ff = hidden.shape
    tokens, width = cotangent.shape
    rank = sketch.shape[2]
    me, y = lax.axis_index("expert"), lax.axis_index("zero")
    z, x, c = me // (nx * nc), me // nc % nx, me % nc
    meta = jnp.stack([z, x, c, y]).astype(jnp.int32)

    def shift(v, dz=0, dx=0, dc=0):
        pairs = []
        for e in range(ne):
            a, b, k = e // (nx * nc), e // nc % nx, e % nc
            to = ((a + dz) % nz * nx + (b + dx) % nx) * nc + (k + dc) % nc
            pairs.append((e, to))
        return lax.ppermute(v, "expert", pairs)

    def shift_y(v, dy):
        return lax.ppermute(v, "zero", [(a, (a + dy) % ny) for a in range(ny)])

    def shaped(s, t=F32):
        return jax.ShapeDtypeStruct(s, t)

    mine = call(
        pack_kernel,
        shaped((tokens, width + tokens), BF),
        (cotangent, gates.T, expert_ids.T),
        specs=[ANY] * 3,
        limit=58 << 20,
        scratch=[
            pltpu.VMEM((gates.shape[1], tokens), F32),
            pltpu.VMEM((gates.shape[1], tokens), jnp.int32),
            pltpu.VMEM((tokens, tokens), BF),
            pltpu.SemaphoreType.DMA((4,)),
        ],
    )

    st = jnp.swapaxes(sketch, 1, 2)
    rows = local * rank
    two = call(sketch_kernel, shaped((2, rows, width), BF), (st.reshape(rows, width),))
    lt = jnp.swapaxes(momentum_left, 1, 2)
    slots = nz * nc * CAP
    count = nx * local
    half = nz // 2

    def along(v, axis="z"):
        pairs = []
        for e in range(ne):
            a, b, k = e // (nx * nc), e // nc % nx, e % nc
            if axis == "z":
                pairs.append((e, ((a + 1 - 2 * k) % nz * nx + b) * nc + k))
            else:
                pairs.append((e, (a * nx + (b - 1 + 2 * k) % nx) * nc + k))
        return lax.ppermute(v, "expert", pairs)

    def swap(v):
        return shift(v, dc=1)

    def project(named, sketches, earlier, parts=1):
        places, blocks = zip(*named)
        nb = len(blocks)
        whole = len(sketches) == 1
        outs = [shaped((count // parts, rank, slots))] * parts
        products = call(
            functools.partial(project_kernel, places, nz, nx, len(earlier), whole),
            outs
            + ([] if whole else [shaped((2 * count * rank, width), BF)])
            + [shaped((2 * nb * count, tokens))],
            (meta, *blocks, *sketches, *earlier),
            specs=[SMEM] + [VMEM] * (nb + len(sketches) + len(earlier)),
            scratch=[pltpu.VMEM((count * rank, nb * tokens), F32)],
            flops=2 * 2 * count * rank * nb * tokens * width,
        )
        return nb, blocks, products[:parts], products[-1], products[-2]

    def ring(k, p, q):
        return [((k, 1), p), ((k, 0), q), ((-k, 0), swap(p)), ((-k, 1), swap(q))]

    lefts = [lt] + [shift_y(lt, d) for d in range(1, ny)]
    left_full, mom = call(
        momentum_kernel,
        [shaped((local, rank, ff))] * 2,
        (meta, st, momentum_right, *lefts),
        specs=[SMEM] + [VMEM] * (2 + ny),
        scratch=[pltpu.VMEM((ny, local, rank, ff // ny), F32)],
    )
    p = along(mine)
    sibling = swap(mine)
    q = along(sibling)
    [p], [q] = after([p], lefts[1]), after([q], lefts[2])
    near = [shift(two, dx=-1), shift(two, dx=1)]
    first = [((0, 1), mine), ((0, 0), sibling)] + ring(1, p, q)
    farther, token = call(
        forward_kernel,
        [shaped((2, rows, width), BF), shaped((8, 128))],
        (meta, *near),
        specs=[SMEM, VMEM, VMEM],
    )
    far = along(farther, "x")
    [p], q = after([along(p)], token, *lefts[3:]), along(q)
    second = ring(2, p, q)
    a = project(first, [two, near[0], far, near[1]], [])
    all_s = [a[4]]
    p, q = along(p), along(q)
    third = ring(3, p, q)
    b = project(second, all_s, a[2])
    [p] = after([along(p)], b[3], mom)
    fourth = [((4, 1), p), ((4, 0), swap(p))]
    e = project(third, all_s, b[2])
    f = project(fourth, all_s, e[2], nx)
    steps = [a, b, e, f]
    counts = [v[0] for v in steps]
    pieces = [block for v in steps for block in v[1]]
    products = [f[2][0]] + [shift(f[2][d], dx=d) for d in range(1, nx)]

    h = hidden.reshape(local, nz, nx, nc * CAP, ff)
    part = call(
        functools.partial(sum_kernel, nx),
        shaped((local, rank, ff)),
        (meta, *products, h, mom),
        specs=[SMEM] + [VMEM] * (nx + 2),
        limit=NARROW,
    )
    parts = [part] + [shift_y(part, d) for d in range(1, ny)]
    basis, *coded = call(
        functools.partial(basis_kernel, ny, nx),
        [shaped((local, rank, ff))] + [shaped((local, rank, slots))] * nx,
        (meta, *parts, h),
        specs=[SMEM] + [VMEM] * (ny + 1),
        limit=NARROW,
    )
    coded = [coded[0]] + [shift(coded[d], dx=d) for d in range(1, nx)]
    coded = [coded[-d % nx] for d in range(nx)]
    own_basis, own_mom = call(
        own_kernel,
        [shaped((local, rank, ff // ny)), shaped(momentum_right.shape)],
        (meta, basis, left_full, momentum_right),
        specs=[SMEM] + [VMEM] * 3,
        limit=NARROW,
    )
    def coefficients(groups, *unread):
        return call(
            functools.partial(
                coefficient_kernel, counts, groups[0] * local, len(groups), len(unread)
            ),
            [shaped((local, rank, width), BF if d else F32) for d in groups],
            (*pieces, *[coded[d] for d in groups], *[v[3] for v in steps], *unread),
            scratch=[pltpu.VMEM((2 * len(groups) * local * rank, sum(counts) * tokens), BF)],
            flops=2 * 2 * len(groups) * local * rank * sum(counts) * tokens * width,
        )

    coeff = coefficients(list(range(nx)), own_mom)
    total = coeff[0]
    for d in range(1, nx):
        total = total + shift(coeff[d], dx=d).astype(F32)
    cols = width // ny

    def columns(d):
        return lax.dynamic_slice_in_dim(total, lax.rem(y + d, ny) * cols, cols, axis=2)

    out = columns(0) + own_mom
    for d in range(1, ny):
        out = out + shift_y(columns(d), d)
    return jnp.swapaxes(own_basis, 1, 2), out


def solution(mesh):
    return jax.shard_map(
        body,
        mesh=mesh,
        in_specs=(
            P(("expert", "zero"), None),
            P(("expert", "zero"), None),
            P(("expert", "zero"), None),
            P("expert", "zero", None),
            P("expert", "zero", None),
            P("expert", None, "zero"),
            P("expert", None, None),
        ),
        out_specs=(P("expert", "zero", None), P("expert", None, "zero")),
        check_vma=False,
    )
```

```python
import functools

import jax
import jax.numpy as jnp
from jax import lax
from jax.experimental import pallas as pl
from jax.experimental.pallas import tpu as pltpu
from jax.sharding import PartitionSpec as P

NX, NC = 4, 2
CAP = 16
MOMENTUM_DECAY = 0.9

WIDE, NARROW = 20 << 20, 8 << 20

BF, F32 = jnp.bfloat16, jnp.float32
HIGHEST = lax.Precision.HIGHEST
VMEM = pl.BlockSpec(memory_space=pltpu.VMEM)
ANY = pl.BlockSpec(memory_space=pl.ANY)
HBM = pl.BlockSpec(memory_space=pltpu.HBM)
SMEM = pl.BlockSpec(memory_space=pltpu.SMEM)
NT = (((1,), (1,)), ((), ()))
NN = (((1,), (0,)), ((), ()))


def dot(a, b, dims=NN, precision=None):
    return lax.dot_general(a, b, dims, precision=precision, preferred_element_type=F32)


def split(v):
    hi = v.astype(BF)
    return hi, (v - hi.astype(F32)).astype(BF)


def stacked(v):
    return jnp.concatenate(split(v), axis=0)


def folded(v):
    half = v.shape[0] // 2
    return v[:half] + v[half:]


def call(kernel, outs, args, specs=None, scratch=(), limit=WIDE, flops=0, spaces=None):
    return pl.pallas_call(
        kernel,
        out_shape=outs,
        in_specs=specs or [VMEM] * len(args),
        out_specs=spaces or jax.tree.map(lambda _: VMEM, outs),
        scratch_shapes=list(scratch),
        compiler_params=pltpu.CompilerParams(vmem_limit_bytes=limit),
        cost_estimate=pl.CostEstimate(flops=flops, bytes_accessed=flops // 500, transcendentals=0),
    )(*args)


def after(values, *needs):
    def kernel(*refs):
        for n in range(len(values)):
            refs[len(values) + len(needs) + n][...] = refs[n][...]

    outs = [jax.ShapeDtypeStruct(v.shape, v.dtype) for v in values]
    return call(kernel, outs, (*values, *needs), limit=NARROW)


def pack_kernel(cot_ref, gates_ref, ids_ref, out_ref, g_scr, i_scr, e_scr, sems):
    tokens, width = cot_ref.shape
    main = pltpu.make_async_copy(cot_ref, out_ref.at[:, 0:width], sems.at[0])
    first = pltpu.make_async_copy(gates_ref, g_scr, sems.at[1])
    second = pltpu.make_async_copy(ids_ref, i_scr, sems.at[2])
    main.start()
    first.start()
    second.start()
    first.wait()
    second.wait()
    g = g_scr[...]
    hi = g.astype(BF).astype(F32)
    mid = (g - hi).astype(BF).astype(F32)
    low = g - hi - mid
    ids = i_scr[...].astype(F32)
    rest = jnp.zeros((tokens - 4 * g.shape[0], tokens), F32)
    e_scr[...] = jnp.concatenate([ids, hi, mid, low, rest], axis=0).astype(BF)
    last = pltpu.make_async_copy(e_scr, out_ref.at[:, width : width + tokens], sems.at[3])
    last.start()
    main.wait()
    last.wait()


def sketch_kernel(st_ref, out_ref):
    hi, low = split(st_ref[...])
    out_ref[0] = hi
    out_ref[1] = low


def momentum_kernel(meta_ref, st_ref, r_ref, *refs):
    lefts, (full_ref, mom_ref, rows) = refs[:-3], refs[-3:]
    ny, y = len(lefts), meta_ref[3]
    for d in range(ny):
        rows[lax.rem(y - d + ny, ny)] = lefts[d][...]
    local = lefts[0].shape[-1]
    cols = r_ref.shape[-1]
    for i in range(r_ref.shape[0]):
        part = st_ref[i, :, pl.ds(pl.multiple_of(y * cols, 128), cols)]
        inner = dot(part, r_ref[i], NT, HIGHEST) * MOMENTUM_DECAY
        for a in range(ny):
            block = rows[a, i]
            full_ref[i, :, a * local : (a + 1) * local] = block
            mom_ref[i, :, a * local : (a + 1) * local] = dot(inner, block, NN, HIGHEST)


def forward_kernel(meta_ref, right_ref, left_ref, out_ref, token_ref):
    out_ref[...] = jnp.where(meta_ref[2] == 0, right_ref[...], left_ref[...])
    token_ref[...] = jnp.zeros_like(token_ref)


def one_hot(place, line):
    return jnp.where(place == line.astype(BF), jnp.ones((), BF), jnp.zeros((), BF))


def project_kernel(places, nz, ng, carried, whole, meta_ref, *refs):
    nb = len(places)
    pieces, refs = refs[:nb], refs[nb:]
    fed = 1 if whole else ng
    sketches, earlier, refs = refs[:fed], refs[fed : fed + carried], refs[fed + carried :]
    outs, (pos_ref, y_scr) = refs[:-2], refs[-2:]
    all_s = sketches[0] if whole else outs[-1]
    outs = outs if whole else outs[:-1]
    _, rank, slots = outs[0].shape
    count = len(outs) * outs[0].shape[0]
    local = count // ng
    rows = count * rank
    gates = nb * count
    tokens = pieces[0].shape[0]
    width = all_s.shape[1]
    if not whole:
        per = rows // ng
        for d in range(ng):
            for k in range(2):
                at = k * rows + d * per
                all_s[at : at + per] = sketches[d][k]
    which = lax.broadcasted_iota(jnp.int32, (count, tokens), 0)
    before = (
        lax.broadcasted_iota(jnp.int32, (tokens, tokens), 0)
        < lax.broadcasted_iota(jnp.int32, (tokens, tokens), 1)
    ).astype(F32).astype(BF)
    z, x, c = meta_ref[0], meta_ref[1], meta_ref[2]
    experts = [
        (((z * NX + lax.rem(x + q // local, ng)) * NC + c) * local + q % local).astype(F32)
        for q in range(count)
    ]
    named, weights = [], []
    for b in range(nb):
        extra = pieces[b][0:32, width:].astype(F32)
        ids = extra[0:8]
        g = extra[8:16] + extra[16:24] + extra[24:32]
        member = jnp.zeros((count, tokens), F32)
        gate = jnp.zeros((count, tokens), F32)
        for q in range(count):
            hit = ids == experts[q]
            m = jnp.sum(jnp.where(hit, 1.0, 0.0), axis=0, keepdims=True)
            w = jnp.sum(jnp.where(hit, g, 0.0), axis=0, keepdims=True)
            member = jnp.where(which == q, m, member)
            gate = jnp.where(which == q, w, gate)
        named.append(member)
        weights.append(gate)
    member = jnp.concatenate(named, axis=0)
    slot = dot(member.astype(BF), before)
    for b, (k, same) in enumerate(places):
        here = slice(b * count, (b + 1) * count)
        source = c if same else NC - 1 - c
        base = ((lax.rem(z - (1 - 2 * c) * k + nz, nz) * NC + source) * CAP).astype(F32)
        pos_ref[here] = jnp.where(member[here] > 0.5, slot[here] + base, -1.0)
        pos_ref[gates + b * count : gates + (b + 1) * count] = weights[b]
    for b in range(0, nb, 2):
        pair = slice(b * tokens, (b + 2) * tokens)
        x2 = jnp.concatenate([ref[:, :width] for ref in pieces[b : b + 2]], axis=0)
        y_scr[:, pair] = folded(dot(all_s[...], x2, NT))
    place = lax.broadcasted_iota(jnp.int32, (slots, nb * tokens), 0).astype(F32).astype(BF)
    for q in range(count):
        line = lambda at: jnp.concatenate(
            [pos_ref[at + b * count + q : at + b * count + q + 1] for b in range(nb)], axis=1
        )
        v = y_scr[q * rank : (q + 1) * rank] * line(gates)
        r = folded(dot(stacked(v), one_hot(place, line(0)), NT))
        per = count // len(outs)
        outs[q // per][q % per] = r + earlier[0][q] if carried else r


def sum_kernel(nd, meta_ref, *refs):
    parts, (h_ref, mom_ref, out_ref) = refs[:nd], refs[nd:]
    for i in range(out_ref.shape[0]):
        total = mom_ref[i]
        for d in range(nd):
            h = h_ref[i, :, lax.rem(meta_ref[1] - d + nd, nd)]
            h = h.reshape(-1, h.shape[-1])
            total = total + folded(dot(stacked(parts[d][i]), h))
        out_ref[i] = total.astype(out_ref.dtype)


def basis_kernel(ny, nd, meta_ref, *refs):
    parts, (h_ref, basis_ref), zs = refs[:ny], refs[ny : ny + 2], refs[ny + 2 :]
    count, rank, ff = basis_ref.shape
    row = lax.broadcasted_iota(jnp.int32, (rank, 2 * rank), 0)
    lane = lax.broadcasted_iota(jnp.int32, (rank, 2 * rank), 1)
    sk, work = [], []
    for i in range(count):
        s = parts[0][i].astype(F32)
        for d in range(1, ny):
            s = s + parts[d][i].astype(F32)
        sk.append(s)
        both = jnp.concatenate([jnp.zeros_like(s), s], axis=0)
        a = dot(s, both, NT, HIGHEST) / ff
        work.append(jnp.where(lane == row, 1.0, a))
    for j in range(rank):
        for i in range(count):
            a = work[i]
            line = a[j : j + 1]
            pivot = jnp.broadcast_to(line[:, rank + j : rank + j + 1], line.shape)
            column = jnp.broadcast_to(a[:, rank + j : rank + j + 1], a.shape)
            work[i] = a - jnp.where(row > j, column, 0.0) * (line / pivot)
    for i in range(count):
        diag = jnp.sum(jnp.where(lane == row + rank, work[i], 0.0), axis=1, keepdims=True)
        inverse = (work[i] / jnp.sqrt(diag))[:, :rank]
        basis = dot(inverse, sk[i], NN, HIGHEST)
        basis_ref[i] = basis
        b = stacked(basis / ff)
        for d in range(nd):
            h = h_ref[i, :, lax.rem(meta_ref[1] + d, nd)]
            h = h.reshape(-1, h.shape[-1])
            zs[d][i] = folded(dot(b, h, NT))


def own_kernel(meta_ref, basis_ref, left_ref, r_ref, out_ref, mom_ref):
    count, rank, ff = basis_ref.shape
    local = out_ref.shape[-1]
    y = meta_ref[3]
    for i in range(count):
        b = basis_ref[i]
        own = b[:, :local]
        for a in range(1, ff // local):
            own = jnp.where(y == a, b[:, a * local : (a + 1) * local], own)
        out_ref[i] = own
        inner = dot(b, left_ref[i], NT, HIGHEST) * (MOMENTUM_DECAY / ff)
        mom_ref[i] = dot(inner, r_ref[i], NN, HIGHEST)


def coefficient_kernel(counts, skipped, nd, unread, *refs):
    nb = sum(counts)
    pieces, refs = refs[:nb], refs[nb:]
    zs, refs = refs[:nd], refs[nd:]
    poss, refs = refs[: len(counts)], refs[len(counts) + unread :]
    outs, w_scr = refs[:nd], refs[nd]
    local, rank, slots = zs[0].shape
    count = nd * local
    every = poss[0].shape[0] // (2 * counts[0])
    tokens = poss[0].shape[1]
    rows = count * rank
    width = outs[0].shape[-1]
    place = lax.broadcasted_iota(jnp.int32, (slots, nb * tokens), 0).astype(F32).astype(BF)
    for q in range(count):
        line = lambda gate: jnp.concatenate(
            [
                r[(gate * n + b) * every + skipped + q : (gate * n + b) * every + skipped + q + 1]
                for r, n in zip(poss, counts)
                for b in range(n)
            ],
            axis=1,
        )
        w = folded(dot(stacked(zs[q // local][q % local]), one_hot(place, line(0)))) * line(1)
        hi, low = split(w)
        w_scr[q * rank : (q + 1) * rank] = hi
        w_scr[rows + q * rank : rows + (q + 1) * rank] = low
    step = 256

    @pl.loop(0, width // step)
    def _(n):
        cols = pl.ds(pl.multiple_of(n * step, step), step)
        x = jnp.concatenate([ref[:, cols] for ref in pieces], axis=0)
        total = folded(dot(w_scr[...], x))
        for q in range(count):
            ref = outs[q // local]
            ref[q % local, :, cols] = total[q * rank : (q + 1) * rank].astype(ref.dtype)


def body(cotangent, gates, expert_ids, hidden, momentum_left, momentum_right, sketch):
    nx, nc = NX, NC
    ne, ny = lax.axis_size("expert"), lax.axis_size("zero")
    nz = ne // (nx * nc)
    local, _, ff = hidden.shape
    tokens, width = cotangent.shape
    rank = sketch.shape[2]
    me, y = lax.axis_index("expert"), lax.axis_index("zero")
    z, x, c = me // (nx * nc), me // nc % nx, me % nc
    meta = jnp.stack([z, x, c, y]).astype(jnp.int32)

    def shift(v, dz=0, dx=0, dc=0):
        pairs = []
        for e in range(ne):
            a, b, k = e // (nx * nc), e // nc % nx, e % nc
            to = ((a + dz) % nz * nx + (b + dx) % nx) * nc + (k + dc) % nc
            pairs.append((e, to))
        return lax.ppermute(v, "expert", pairs)

    def shift_y(v, dy):
        return lax.ppermute(v, "zero", [(a, (a + dy) % ny) for a in range(ny)])

    def shaped(s, t=F32):
        return jax.ShapeDtypeStruct(s, t)

    mine = call(
        pack_kernel,
        shaped((tokens, width + tokens), BF),
        (cotangent, gates.T, expert_ids.T),
        specs=[ANY] * 3,
        limit=58 << 20,
        scratch=[
            pltpu.VMEM((gates.shape[1], tokens), F32),
            pltpu.VMEM((gates.shape[1], tokens), jnp.int32),
            pltpu.VMEM((tokens, tokens), BF),
            pltpu.SemaphoreType.DMA((4,)),
        ],
    )

    st = jnp.swapaxes(sketch, 1, 2)
    rows = local * rank
    two = call(sketch_kernel, shaped((2, rows, width), BF), (st.reshape(rows, width),))
    lt = jnp.swapaxes(momentum_left, 1, 2)
    slots = nz * nc * CAP
    count = nx * local
    half = nz // 2

    def along(v, axis="z"):
        pairs = []
        for e in range(ne):
            a, b, k = e // (nx * nc), e // nc % nx, e % nc
            if axis == "z":
                pairs.append((e, ((a + 1 - 2 * k) % nz * nx + b) * nc + k))
            else:
                pairs.append((e, (a * nx + (b - 1 + 2 * k) % nx) * nc + k))
        return lax.ppermute(v, "expert", pairs)

    def swap(v):
        return shift(v, dc=1)

    def project(named, sketches, earlier, parts=1):
        places, blocks = zip(*named)
        nb = len(blocks)
        whole = len(sketches) == 1
        outs = [shaped((count // parts, rank, slots))] * parts
        products = call(
            functools.partial(project_kernel, places, nz, nx, len(earlier), whole),
            outs
            + ([] if whole else [shaped((2 * count * rank, width), BF)])
            + [shaped((2 * nb * count, tokens))],
            (meta, *blocks, *sketches, *earlier),
            specs=[SMEM] + [VMEM] * (nb + len(sketches) + len(earlier)),
            scratch=[pltpu.VMEM((count * rank, nb * tokens), F32)],
            flops=2 * 2 * count * rank * nb * tokens * width,
        )
        return nb, blocks, products[:parts], products[-1], products[-2]

    def ring(k, p, q):
        return [((k, 1), p), ((k, 0), q), ((-k, 0), swap(p)), ((-k, 1), swap(q))]

    lefts = [lt] + [shift_y(lt, d) for d in range(1, ny)]
    left_full, mom = call(
        momentum_kernel,
        [shaped((local, rank, ff))] * 2,
        (meta, st, momentum_right, *lefts),
        specs=[SMEM] + [VMEM] * (2 + ny),
        scratch=[pltpu.VMEM((ny, local, rank, ff // ny), F32)],
    )
    p = along(mine)
    sibling = swap(mine)
    q = along(sibling)
    [p], [q] = after([p], lefts[1]), after([q], lefts[2])
    near = [shift(two, dx=-1), shift(two, dx=1)]
    first = [((0, 1), mine), ((0, 0), sibling)] + ring(1, p, q)
    farther, token = call(
        forward_kernel,
        [shaped((2, rows, width), BF), shaped((8, 128))],
        (meta, *near),
        specs=[SMEM, VMEM, VMEM],
    )
    far = along(farther, "x")
    [p], q = after([along(p)], token, *lefts[3:]), along(q)
    second = ring(2, p, q)
    a = project(first, [two, near[0], far, near[1]], [])
    all_s = [a[4]]
    p, q = along(p), along(q)
    third = ring(3, p, q)
    b = project(second, all_s, a[2])
    [p] = after([along(p)], b[3], mom)
    fourth = [((4, 1), p), ((4, 0), swap(p))]
    e = project(third, all_s, b[2])
    f = project(fourth, all_s, e[2], nx)
    steps = [a, b, e, f]
    counts = [v[0] for v in steps]
    pieces = [block for v in steps for block in v[1]]
    products = [f[2][0]] + [shift(f[2][d], dx=d) for d in range(1, nx)]

    h = hidden.reshape(local, nz, nx, nc * CAP, ff)
    part = call(
        functools.partial(sum_kernel, nx),
        shaped((local, rank, ff), BF),
        (meta, *products, h, mom),
        specs=[SMEM] + [VMEM] * (nx + 2),
        limit=NARROW,
    )
    parts = [part] + [shift_y(part, d) for d in range(1, ny)]
    basis, *coded = call(
        functools.partial(basis_kernel, ny, nx),
        [shaped((local, rank, ff))] + [shaped((local, rank, slots))] * nx,
        (meta, *parts, h),
        specs=[SMEM] + [VMEM] * (ny + 1),
        limit=NARROW,
    )
    coded = [coded[0]] + [shift(coded[d], dx=d) for d in range(1, nx)]
    coded = [coded[-d % nx] for d in range(nx)]
    own_basis, own_mom = call(
        own_kernel,
        [shaped((local, rank, ff // ny)), shaped(momentum_right.shape)],
        (meta, basis, left_full, momentum_right),
        specs=[SMEM] + [VMEM] * 3,
        limit=NARROW,
    )
    def coefficients(groups, *unread):
        return call(
            functools.partial(
                coefficient_kernel, counts, groups[0] * local, len(groups), len(unread)
            ),
            [shaped((local, rank, width), BF if d else F32) for d in groups],
            (*pieces, *[coded[d] for d in groups], *[v[3] for v in steps], *unread),
            scratch=[pltpu.VMEM((2 * len(groups) * local * rank, sum(counts) * tokens), BF)],
            flops=2 * 2 * len(groups) * local * rank * sum(counts) * tokens * width,
        )

    coeff = coefficients(list(range(nx)), own_mom)
    total = coeff[0]
    for d in range(1, nx):
        total = total + shift(coeff[d], dx=d).astype(F32)
    cols = width // ny

    def columns(d):
        return lax.dynamic_slice_in_dim(total, lax.rem(y + d, ny) * cols, cols, axis=2)

    out = columns(0) + own_mom
    for d in range(1, ny):
        out = out + shift_y(columns(d), d)
    return jnp.swapaxes(own_basis, 1, 2), out


def solution(mesh):
    return jax.shard_map(
        body,
        mesh=mesh,
        in_specs=(
            P(("expert", "zero"), None),
            P(("expert", "zero"), None),
            P(("expert", "zero"), None),
            P("expert", "zero", None),
            P("expert", "zero", None),
            P("expert", None, "zero"),
            P("expert", None, None),
        ),
        out_specs=(P("expert", "zero", None), P("expert", None, "zero")),
        check_vma=False,
    )
```

```python
import functools

import jax
import jax.numpy as jnp
from jax import lax
from jax.experimental import pallas as pl
from jax.experimental.pallas import tpu as pltpu
from jax.sharding import PartitionSpec as P

NX, NC = 4, 2
CAP = 16
MOMENTUM_DECAY = 0.9

WIDE, NARROW = 20 << 20, 8 << 20

BF, F32 = jnp.bfloat16, jnp.float32
HIGHEST = lax.Precision.HIGHEST
VMEM = pl.BlockSpec(memory_space=pltpu.VMEM)
ANY = pl.BlockSpec(memory_space=pl.ANY)
HBM = pl.BlockSpec(memory_space=pltpu.HBM)
SMEM = pl.BlockSpec(memory_space=pltpu.SMEM)
NT = (((1,), (1,)), ((), ()))
NN = (((1,), (0,)), ((), ()))


def dot(a, b, dims=NN, precision=None):
    return lax.dot_general(a, b, dims, precision=precision, preferred_element_type=F32)


def split(v):
    hi = v.astype(BF)
    return hi, (v - hi.astype(F32)).astype(BF)


def stacked(v):
    return jnp.concatenate(split(v), axis=0)


def folded(v):
    half = v.shape[0] // 2
    return v[:half] + v[half:]


def call(kernel, outs, args, specs=None, scratch=(), limit=WIDE, flops=0, spaces=None):
    return pl.pallas_call(
        kernel,
        out_shape=outs,
        in_specs=specs or [VMEM] * len(args),
        out_specs=spaces or jax.tree.map(lambda _: VMEM, outs),
        scratch_shapes=list(scratch),
        compiler_params=pltpu.CompilerParams(vmem_limit_bytes=limit),
        cost_estimate=pl.CostEstimate(flops=flops, bytes_accessed=flops // 500, transcendentals=0),
    )(*args)


def after(values, *needs):
    def kernel(*refs):
        for n in range(len(values)):
            refs[len(values) + len(needs) + n][...] = refs[n][...]

    outs = [jax.ShapeDtypeStruct(v.shape, v.dtype) for v in values]
    return call(kernel, outs, (*values, *needs), limit=NARROW)


def pack_kernel(cot_ref, gates_ref, ids_ref, out_ref, g_scr, i_scr, e_scr, sems):
    tokens, width = cot_ref.shape
    main = pltpu.make_async_copy(cot_ref, out_ref.at[:, 0:width], sems.at[0])
    first = pltpu.make_async_copy(gates_ref, g_scr, sems.at[1])
    second = pltpu.make_async_copy(ids_ref, i_scr, sems.at[2])
    main.start()
    first.start()
    second.start()
    first.wait()
    second.wait()
    g = g_scr[...]
    hi = g.astype(BF).astype(F32)
    mid = (g - hi).astype(BF).astype(F32)
    low = g - hi - mid
    ids = i_scr[...].astype(F32)
    rest = jnp.zeros((tokens - 4 * g.shape[0], tokens), F32)
    e_scr[...] = jnp.concatenate([ids, hi, mid, low, rest], axis=0).astype(BF)
    last = pltpu.make_async_copy(e_scr, out_ref.at[:, width : width + tokens], sems.at[3])
    last.start()
    main.wait()
    last.wait()


def sketch_kernel(st_ref, out_ref):
    hi, low = split(st_ref[...])
    out_ref[0] = hi
    out_ref[1] = low


def momentum_kernel(meta_ref, st_ref, r_ref, *refs):
    lefts, (full_ref, mom_ref, rows) = refs[:-3], refs[-3:]
    ny, y = len(lefts), meta_ref[3]
    for d in range(ny):
        rows[lax.rem(y - d + ny, ny)] = lefts[d][...]
    local = lefts[0].shape[-1]
    cols = r_ref.shape[-1]
    for i in range(r_ref.shape[0]):
        part = st_ref[i, :, pl.ds(pl.multiple_of(y * cols, 128), cols)]
        inner = dot(part, r_ref[i], NT, HIGHEST) * MOMENTUM_DECAY
        for a in range(ny):
            block = rows[a, i]
            full_ref[i, :, a * local : (a + 1) * local] = block
            mom_ref[i, :, a * local : (a + 1) * local] = dot(inner, block, NN, HIGHEST)


def forward_kernel(meta_ref, right_ref, left_ref, out_ref, token_ref):
    out_ref[...] = jnp.where(meta_ref[2] == 0, right_ref[...], left_ref[...])
    token_ref[...] = jnp.zeros_like(token_ref)


def one_hot(place, line):
    return jnp.where(place == line.astype(BF), jnp.ones((), BF), jnp.zeros((), BF))


def project_kernel(places, nz, ng, carried, whole, meta_ref, *refs):
    nb = len(places)
    pieces, refs = refs[:nb], refs[nb:]
    fed = 1 if whole else ng
    sketches, earlier, refs = refs[:fed], refs[fed : fed + carried], refs[fed + carried :]
    outs, (pos_ref, y_scr) = refs[:-2], refs[-2:]
    all_s = sketches[0] if whole else outs[-1]
    outs = outs if whole else outs[:-1]
    _, rank, slots = outs[0].shape
    count = len(outs) * outs[0].shape[0]
    local = count // ng
    rows = count * rank
    gates = nb * count
    tokens = pieces[0].shape[0]
    width = all_s.shape[1]
    if not whole:
        per = rows // ng
        for d in range(ng):
            for k in range(2):
                at = k * rows + d * per
                all_s[at : at + per] = sketches[d][k]
    which = lax.broadcasted_iota(jnp.int32, (count, tokens), 0)
    before = (
        lax.broadcasted_iota(jnp.int32, (tokens, tokens), 0)
        < lax.broadcasted_iota(jnp.int32, (tokens, tokens), 1)
    ).astype(F32).astype(BF)
    z, x, c = meta_ref[0], meta_ref[1], meta_ref[2]
    experts = [
        (((z * NX + lax.rem(x + q // local, ng)) * NC + c) * local + q % local).astype(F32)
        for q in range(count)
    ]
    named, weights = [], []
    for b in range(nb):
        extra = pieces[b][0:32, width:].astype(F32)
        ids = extra[0:8]
        g = extra[8:16] + extra[16:24] + extra[24:32]
        member = jnp.zeros((count, tokens), F32)
        gate = jnp.zeros((count, tokens), F32)
        for q in range(count):
            hit = ids == experts[q]
            m = jnp.sum(jnp.where(hit, 1.0, 0.0), axis=0, keepdims=True)
            w = jnp.sum(jnp.where(hit, g, 0.0), axis=0, keepdims=True)
            member = jnp.where(which == q, m, member)
            gate = jnp.where(which == q, w, gate)
        named.append(member)
        weights.append(gate)
    member = jnp.concatenate(named, axis=0)
    slot = dot(member.astype(BF), before)
    for b, (k, same) in enumerate(places):
        here = slice(b * count, (b + 1) * count)
        source = c if same else NC - 1 - c
        base = ((lax.rem(z - (1 - 2 * c) * k + nz, nz) * NC + source) * CAP).astype(F32)
        pos_ref[here] = jnp.where(member[here] > 0.5, slot[here] + base, -1.0)
        pos_ref[gates + b * count : gates + (b + 1) * count] = weights[b]
    for b in range(0, nb, 2):
        pair = slice(b * tokens, (b + 2) * tokens)
        x2 = jnp.concatenate([ref[:, :width] for ref in pieces[b : b + 2]], axis=0)
        y_scr[:, pair] = folded(dot(all_s[...], x2, NT))
    place = lax.broadcasted_iota(jnp.int32, (slots, nb * tokens), 0).astype(F32).astype(BF)
    for q in range(count):
        line = lambda at: jnp.concatenate(
            [pos_ref[at + b * count + q : at + b * count + q + 1] for b in range(nb)], axis=1
        )
        v = y_scr[q * rank : (q + 1) * rank] * line(gates)
        r = folded(dot(stacked(v), one_hot(place, line(0)), NT))
        per = count // len(outs)
        outs[q // per][q % per] = r + earlier[0][q] if carried else r


def sum_kernel(nd, meta_ref, *refs):
    parts, (h_ref, mom_ref, out_ref) = refs[:nd], refs[nd:]
    for i in range(out_ref.shape[0]):
        total = mom_ref[i]
        for d in range(nd):
            h = h_ref[i, :, lax.rem(meta_ref[1] - d + nd, nd)]
            h = h.reshape(-1, h.shape[-1])
            total = total + folded(dot(stacked(parts[d][i]), h))
        out_ref[i] = total.astype(out_ref.dtype)


def basis_kernel(ny, nd, meta_ref, *refs):
    parts, (h_ref, basis_ref), zs = refs[:ny], refs[ny : ny + 2], refs[ny + 2 :]
    count, rank, ff = basis_ref.shape
    row = lax.broadcasted_iota(jnp.int32, (rank, 2 * rank), 0)
    lane = lax.broadcasted_iota(jnp.int32, (rank, 2 * rank), 1)
    sk, work = [], []
    for i in range(count):
        s = parts[0][i].astype(F32)
        for d in range(1, ny):
            s = s + parts[d][i].astype(F32)
        sk.append(s)
        both = jnp.concatenate([jnp.zeros_like(s), s], axis=0)
        a = dot(s, both, NT, HIGHEST) / ff
        work.append(jnp.where(lane == row, 1.0, a))
    for j in range(rank):
        for i in range(count):
            a = work[i]
            line = a[j : j + 1]
            pivot = jnp.broadcast_to(line[:, rank + j : rank + j + 1], line.shape)
            column = jnp.broadcast_to(a[:, rank + j : rank + j + 1], a.shape)
            work[i] = a - jnp.where(row > j, column, 0.0) * (line / pivot)
    for i in range(count):
        diag = jnp.sum(jnp.where(lane == row + rank, work[i], 0.0), axis=1, keepdims=True)
        inverse = (work[i] / jnp.sqrt(diag))[:, :rank]
        basis = dot(inverse, sk[i], NN, HIGHEST)
        basis_ref[i] = basis
        b = stacked(basis / ff)
        for d in range(nd):
            h = h_ref[i, :, lax.rem(meta_ref[1] + d, nd)]
            h = h.reshape(-1, h.shape[-1])
            zs[d][i] = folded(dot(b, h, NT))


def own_kernel(meta_ref, basis_ref, left_ref, r_ref, out_ref, mom_ref):
    count, rank, ff = basis_ref.shape
    local = out_ref.shape[-1]
    y = meta_ref[3]
    for i in range(count):
        b = basis_ref[i]
        own = b[:, :local]
        for a in range(1, ff // local):
            own = jnp.where(y == a, b[:, a * local : (a + 1) * local], own)
        out_ref[i] = own
        inner = dot(b, left_ref[i], NT, HIGHEST) * (MOMENTUM_DECAY / ff)
        mom_ref[i] = dot(inner, r_ref[i], NN, HIGHEST)


def coefficient_kernel(counts, skipped, nd, unread, *refs):
    nb = sum(counts)
    pieces, refs = refs[:nb], refs[nb:]
    zs, refs = refs[:nd], refs[nd:]
    poss, refs = refs[: len(counts)], refs[len(counts) + unread :]
    outs, w_scr = refs[:nd], refs[nd]
    local, rank, slots = zs[0].shape
    count = nd * local
    every = poss[0].shape[0] // (2 * counts[0])
    tokens = poss[0].shape[1]
    rows = count * rank
    width = outs[0].shape[-1]
    place = lax.broadcasted_iota(jnp.int32, (slots, nb * tokens), 0).astype(F32).astype(BF)
    for q in range(count):
        line = lambda gate: jnp.concatenate(
            [
                r[(gate * n + b) * every + skipped + q : (gate * n + b) * every + skipped + q + 1]
                for r, n in zip(poss, counts)
                for b in range(n)
            ],
            axis=1,
        )
        w = folded(dot(stacked(zs[q // local][q % local]), one_hot(place, line(0)))) * line(1)
        hi, low = split(w)
        w_scr[q * rank : (q + 1) * rank] = hi
        w_scr[rows + q * rank : rows + (q + 1) * rank] = low
    step = 256

    @pl.loop(0, width // step)
    def _(n):
        cols = pl.ds(pl.multiple_of(n * step, step), step)
        x = jnp.concatenate([ref[:, cols] for ref in pieces], axis=0)
        total = folded(dot(w_scr[...], x))
        for q in range(count):
            ref = outs[q // local]
            ref[q % local, :, cols] = total[q * rank : (q + 1) * rank].astype(ref.dtype)


def body(cotangent, gates, expert_ids, hidden, momentum_left, momentum_right, sketch):
    nx, nc = NX, NC
    ne, ny = lax.axis_size("expert"), lax.axis_size("zero")
    nz = ne // (nx * nc)
    local, _, ff = hidden.shape
    tokens, width = cotangent.shape
    rank = sketch.shape[2]
    me, y = lax.axis_index("expert"), lax.axis_index("zero")
    z, x, c = me // (nx * nc), me // nc % nx, me % nc
    meta = jnp.stack([z, x, c, y]).astype(jnp.int32)

    def shift(v, dz=0, dx=0, dc=0):
        pairs = []
        for e in range(ne):
            a, b, k = e // (nx * nc), e // nc % nx, e % nc
            to = ((a + dz) % nz * nx + (b + dx) % nx) * nc + (k + dc) % nc
            pairs.append((e, to))
        return lax.ppermute(v, "expert", pairs)

    def shift_y(v, dy):
        return lax.ppermute(v, "zero", [(a, (a + dy) % ny) for a in range(ny)])

    def shaped(s, t=F32):
        return jax.ShapeDtypeStruct(s, t)

    mine = call(
        pack_kernel,
        shaped((tokens, width + tokens), BF),
        (cotangent, gates.T, expert_ids.T),
        specs=[ANY] * 3,
        limit=58 << 20,
        scratch=[
            pltpu.VMEM((gates.shape[1], tokens), F32),
            pltpu.VMEM((gates.shape[1], tokens), jnp.int32),
            pltpu.VMEM((tokens, tokens), BF),
            pltpu.SemaphoreType.DMA((4,)),
        ],
    )

    st = jnp.swapaxes(sketch, 1, 2)
    rows = local * rank
    two = call(sketch_kernel, shaped((2, rows, width), BF), (st.reshape(rows, width),))
    lt = jnp.swapaxes(momentum_left, 1, 2)
    slots = nz * nc * CAP
    count = nx * local
    half = nz // 2

    def along(v, axis="z"):
        pairs = []
        for e in range(ne):
            a, b, k = e // (nx * nc), e // nc % nx, e % nc
            if axis == "z":
                pairs.append((e, ((a + 1 - 2 * k) % nz * nx + b) * nc + k))
            else:
                pairs.append((e, (a * nx + (b - 1 + 2 * k) % nx) * nc + k))
        return lax.ppermute(v, "expert", pairs)

    def swap(v):
        return shift(v, dc=1)

    def project(named, sketches, earlier, parts=1):
        places, blocks = zip(*named)
        nb = len(blocks)
        whole = len(sketches) == 1
        outs = [shaped((count // parts, rank, slots))] * parts
        products = call(
            functools.partial(project_kernel, places, nz, nx, len(earlier), whole),
            outs
            + ([] if whole else [shaped((2 * count * rank, width), BF)])
            + [shaped((2 * nb * count, tokens))],
            (meta, *blocks, *sketches, *earlier),
            specs=[SMEM] + [VMEM] * (nb + len(sketches) + len(earlier)),
            scratch=[pltpu.VMEM((count * rank, nb * tokens), F32)],
            flops=2 * 2 * count * rank * nb * tokens * width,
        )
        return nb, blocks, products[:parts], products[-1], products[-2]

    def ring(k, p, q):
        return [((k, 1), p), ((k, 0), q), ((-k, 0), swap(p)), ((-k, 1), swap(q))]

    lefts = [lt] + [shift_y(lt, d) for d in range(1, ny)]
    left_full, mom = call(
        momentum_kernel,
        [shaped((local, rank, ff))] * 2,
        (meta, st, momentum_right, *lefts),
        specs=[SMEM] + [VMEM] * (2 + ny),
        scratch=[pltpu.VMEM((ny, local, rank, ff // ny), F32)],
    )
    p = along(mine)
    sibling = swap(mine)
    q = along(sibling)
    [p], [q] = after([p], lefts[1]), after([q], lefts[2])
    near = [shift(two, dx=-1), shift(two, dx=1)]
    first = [((0, 1), mine), ((0, 0), sibling)] + ring(1, p, q)
    farther, token = call(
        forward_kernel,
        [shaped((2, rows, width), BF), shaped((8, 128))],
        (meta, *near),
        specs=[SMEM, VMEM, VMEM],
    )
    far = along(farther, "x")
    p, [q] = along(p), after([along(q)], token, *lefts[3:])
    second = ring(2, p, q)
    a = project(first, [two, near[0], far, near[1]], [])
    all_s = [a[4]]
    p, q = along(p), along(q)
    third = ring(3, p, q)
    b = project(second, all_s, a[2])
    [p] = after([along(p)], b[3], mom)
    fourth = [((4, 1), p), ((4, 0), swap(p))]
    e = project(third, all_s, b[2])
    f = project(fourth, all_s, e[2], nx)
    steps = [a, b, e, f]
    counts = [v[0] for v in steps]
    pieces = [block for v in steps for block in v[1]]
    products = [f[2][0]] + [shift(f[2][d], dx=d) for d in range(1, nx)]

    h = hidden.reshape(local, nz, nx, nc * CAP, ff)
    part = call(
        functools.partial(sum_kernel, nx),
        shaped((local, rank, ff), BF),
        (meta, *products, h, mom),
        specs=[SMEM] + [VMEM] * (nx + 2),
        limit=NARROW,
    )
    parts = [part] + [shift_y(part, d) for d in range(1, ny)]
    basis, *coded = call(
        functools.partial(basis_kernel, ny, nx),
        [shaped((local, rank, ff))] + [shaped((local, rank, slots))] * nx,
        (meta, *parts, h),
        specs=[SMEM] + [VMEM] * (ny + 1),
        limit=NARROW,
    )
    coded = [coded[0]] + [shift(coded[d], dx=d) for d in range(1, nx)]
    coded = [coded[-d % nx] for d in range(nx)]
    own_basis, own_mom = call(
        own_kernel,
        [shaped((local, rank, ff // ny)), shaped(momentum_right.shape)],
        (meta, basis, left_full, momentum_right),
        specs=[SMEM] + [VMEM] * 3,
        limit=NARROW,
    )
    def coefficients(groups, *unread):
        return call(
            functools.partial(
                coefficient_kernel, counts, groups[0] * local, len(groups), len(unread)
            ),
            [shaped((local, rank, width), BF if d else F32) for d in groups],
            (*pieces, *[coded[d] for d in groups], *[v[3] for v in steps], *unread),
            scratch=[pltpu.VMEM((2 * len(groups) * local * rank, sum(counts) * tokens), BF)],
            flops=2 * 2 * len(groups) * local * rank * sum(counts) * tokens * width,
        )

    coeff = coefficients(list(range(nx)), own_mom)
    total = coeff[0]
    for d in range(1, nx):
        total = total + shift(coeff[d], dx=d).astype(F32)
    cols = width // ny

    def columns(d):
        return lax.dynamic_slice_in_dim(total, lax.rem(y + d, ny) * cols, cols, axis=2)

    out = columns(0) + own_mom
    for d in range(1, ny):
        out = out + shift_y(columns(d), d)
    return jnp.swapaxes(own_basis, 1, 2), out


def solution(mesh):
    return jax.shard_map(
        body,
        mesh=mesh,
        in_specs=(
            P(("expert", "zero"), None),
            P(("expert", "zero"), None),
            P(("expert", "zero"), None),
            P("expert", "zero", None),
            P("expert", "zero", None),
            P("expert", None, "zero"),
            P("expert", None, None),
        ),
        out_specs=(P("expert", "zero", None), P("expert", None, "zero")),
        check_vma=False,
    )
```

```python
import functools

import jax
import jax.numpy as jnp
from jax import lax
from jax.experimental import pallas as pl
from jax.experimental.pallas import tpu as pltpu
from jax.sharding import PartitionSpec as P

NX, NC = 4, 2
CAP = 16
MOMENTUM_DECAY = 0.9

WIDE, NARROW = 20 << 20, 8 << 20

BF, F32 = jnp.bfloat16, jnp.float32
HIGHEST = lax.Precision.HIGHEST
VMEM = pl.BlockSpec(memory_space=pltpu.VMEM)
ANY = pl.BlockSpec(memory_space=pl.ANY)
HBM = pl.BlockSpec(memory_space=pltpu.HBM)
SMEM = pl.BlockSpec(memory_space=pltpu.SMEM)
NT = (((1,), (1,)), ((), ()))
NN = (((1,), (0,)), ((), ()))


def dot(a, b, dims=NN, precision=None):
    return lax.dot_general(a, b, dims, precision=precision, preferred_element_type=F32)


def split(v):
    hi = v.astype(BF)
    return hi, (v - hi.astype(F32)).astype(BF)


def stacked(v):
    return jnp.concatenate(split(v), axis=0)


def folded(v):
    half = v.shape[0] // 2
    return v[:half] + v[half:]


def call(kernel, outs, args, specs=None, scratch=(), limit=WIDE, flops=0, spaces=None):
    return pl.pallas_call(
        kernel,
        out_shape=outs,
        in_specs=specs or [VMEM] * len(args),
        out_specs=spaces or jax.tree.map(lambda _: VMEM, outs),
        scratch_shapes=list(scratch),
        compiler_params=pltpu.CompilerParams(vmem_limit_bytes=limit),
        cost_estimate=pl.CostEstimate(flops=flops, bytes_accessed=flops // 500, transcendentals=0),
    )(*args)


def after(values, *needs):
    def kernel(*refs):
        for n in range(len(values)):
            refs[len(values) + len(needs) + n][...] = refs[n][...]

    outs = [jax.ShapeDtypeStruct(v.shape, v.dtype) for v in values]
    return call(kernel, outs, (*values, *needs), limit=NARROW)


def pack_kernel(cot_ref, gates_ref, ids_ref, out_ref, g_scr, i_scr, e_scr, sems):
    tokens, width = cot_ref.shape
    main = pltpu.make_async_copy(cot_ref, out_ref.at[:, 0:width], sems.at[0])
    first = pltpu.make_async_copy(gates_ref, g_scr, sems.at[1])
    second = pltpu.make_async_copy(ids_ref, i_scr, sems.at[2])
    main.start()
    first.start()
    second.start()
    first.wait()
    second.wait()
    g = g_scr[...]
    hi = g.astype(BF).astype(F32)
    mid = (g - hi).astype(BF).astype(F32)
    low = g - hi - mid
    ids = i_scr[...].astype(F32)
    rest = jnp.zeros((tokens - 4 * g.shape[0], tokens), F32)
    e_scr[...] = jnp.concatenate([ids, hi, mid, low, rest], axis=0).astype(BF)
    last = pltpu.make_async_copy(e_scr, out_ref.at[:, width : width + tokens], sems.at[3])
    last.start()
    main.wait()
    last.wait()


def sketch_kernel(st_ref, out_ref):
    hi, low = split(st_ref[...])
    out_ref[0] = hi
    out_ref[1] = low


def momentum_kernel(meta_ref, st_ref, r_ref, *refs):
    lefts, (full_ref, mom_ref, rows) = refs[:-3], refs[-3:]
    ny, y = len(lefts), meta_ref[3]
    for d in range(ny):
        rows[lax.rem(y - d + ny, ny)] = lefts[d][...]
    local = lefts[0].shape[-1]
    cols = r_ref.shape[-1]
    for i in range(r_ref.shape[0]):
        part = st_ref[i, :, pl.ds(pl.multiple_of(y * cols, 128), cols)]
        inner = dot(part, r_ref[i], NT, HIGHEST) * MOMENTUM_DECAY
        for a in range(ny):
            block = rows[a, i]
            full_ref[i, :, a * local : (a + 1) * local] = block
            mom_ref[i, :, a * local : (a + 1) * local] = dot(inner, block, NN, HIGHEST)


def forward_kernel(meta_ref, right_ref, left_ref, out_ref, token_ref):
    out_ref[...] = jnp.where(meta_ref[2] == 0, right_ref[...], left_ref[...])
    token_ref[...] = jnp.zeros_like(token_ref)


def one_hot(place, line):
    return jnp.where(place == line.astype(BF), jnp.ones((), BF), jnp.zeros((), BF))


def project_kernel(places, nz, ng, carried, whole, meta_ref, *refs):
    nb = len(places)
    pieces, refs = refs[:nb], refs[nb:]
    fed = 1 if whole else ng
    sketches, earlier, refs = refs[:fed], refs[fed : fed + carried], refs[fed + carried :]
    outs, (pos_ref, y_scr) = refs[:-2], refs[-2:]
    all_s = sketches[0] if whole else outs[-1]
    outs = outs if whole else outs[:-1]
    _, rank, slots = outs[0].shape
    count = len(outs) * outs[0].shape[0]
    local = count // ng
    rows = count * rank
    gates = nb * count
    tokens = pieces[0].shape[0]
    width = all_s.shape[1]
    if not whole:
        per = rows // ng
        for d in range(ng):
            for k in range(2):
                at = k * rows + d * per
                all_s[at : at + per] = sketches[d][k]
    which = lax.broadcasted_iota(jnp.int32, (count, tokens), 0)
    before = (
        lax.broadcasted_iota(jnp.int32, (tokens, tokens), 0)
        < lax.broadcasted_iota(jnp.int32, (tokens, tokens), 1)
    ).astype(F32).astype(BF)
    z, x, c = meta_ref[0], meta_ref[1], meta_ref[2]
    experts = [
        (((z * NX + lax.rem(x + q // local, ng)) * NC + c) * local + q % local).astype(F32)
        for q in range(count)
    ]
    named, weights = [], []
    for b in range(nb):
        extra = pieces[b][0:32, width:].astype(F32)
        ids = extra[0:8]
        g = extra[8:16] + extra[16:24] + extra[24:32]
        member = jnp.zeros((count, tokens), F32)
        gate = jnp.zeros((count, tokens), F32)
        for q in range(count):
            hit = ids == experts[q]
            m = jnp.sum(jnp.where(hit, 1.0, 0.0), axis=0, keepdims=True)
            w = jnp.sum(jnp.where(hit, g, 0.0), axis=0, keepdims=True)
            member = jnp.where(which == q, m, member)
            gate = jnp.where(which == q, w, gate)
        named.append(member)
        weights.append(gate)
    member = jnp.concatenate(named, axis=0)
    slot = dot(member.astype(BF), before)
    for b, (k, same) in enumerate(places):
        here = slice(b * count, (b + 1) * count)
        source = c if same else NC - 1 - c
        base = ((lax.rem(z - (1 - 2 * c) * k + nz, nz) * NC + source) * CAP).astype(F32)
        pos_ref[here] = jnp.where(member[here] > 0.5, slot[here] + base, -1.0)
        pos_ref[gates + b * count : gates + (b + 1) * count] = weights[b]
    for b in range(0, nb, 2):
        pair = slice(b * tokens, (b + 2) * tokens)
        x2 = jnp.concatenate([ref[:, :width] for ref in pieces[b : b + 2]], axis=0)
        y_scr[:, pair] = folded(dot(all_s[...], x2, NT))
    place = lax.broadcasted_iota(jnp.int32, (slots, nb * tokens), 0).astype(F32).astype(BF)
    for q in range(count):
        line = lambda at: jnp.concatenate(
            [pos_ref[at + b * count + q : at + b * count + q + 1] for b in range(nb)], axis=1
        )
        v = y_scr[q * rank : (q + 1) * rank] * line(gates)
        r = folded(dot(stacked(v), one_hot(place, line(0)), NT))
        per = count // len(outs)
        outs[q // per][q % per] = r + earlier[0][q] if carried else r


def sum_kernel(nd, meta_ref, *refs):
    parts, (h_ref, mom_ref, out_ref) = refs[:nd], refs[nd:]
    for i in range(out_ref.shape[0]):
        total = mom_ref[i]
        for d in range(nd):
            h = h_ref[i, :, lax.rem(meta_ref[1] - d + nd, nd)]
            h = h.reshape(-1, h.shape[-1])
            total = total + folded(dot(stacked(parts[d][i]), h))
        out_ref[i] = total.astype(out_ref.dtype)


def basis_kernel(ny, nd, meta_ref, *refs):
    parts, (h_ref, basis_ref), zs = refs[:ny], refs[ny : ny + 2], refs[ny + 2 :]
    count, rank, ff = basis_ref.shape
    row = lax.broadcasted_iota(jnp.int32, (rank, 2 * rank), 0)
    lane = lax.broadcasted_iota(jnp.int32, (rank, 2 * rank), 1)
    sk, work = [], []
    for i in range(count):
        s = parts[0][i].astype(F32)
        for d in range(1, ny):
            s = s + parts[d][i].astype(F32)
        sk.append(s)
        both = jnp.concatenate([jnp.zeros_like(s), s], axis=0)
        a = dot(s, both, NT, HIGHEST) / ff
        work.append(jnp.where(lane == row, 1.0, a))
    for j in range(rank):
        for i in range(count):
            a = work[i]
            line = a[j : j + 1]
            pivot = jnp.broadcast_to(line[:, rank + j : rank + j + 1], line.shape)
            column = jnp.broadcast_to(a[:, rank + j : rank + j + 1], a.shape)
            work[i] = a - jnp.where(row > j, column, 0.0) * (line / pivot)
    for i in range(count):
        diag = jnp.sum(jnp.where(lane == row + rank, work[i], 0.0), axis=1, keepdims=True)
        inverse = (work[i] / jnp.sqrt(diag))[:, :rank]
        basis = dot(inverse, sk[i], NN, HIGHEST)
        basis_ref[i] = basis
        hi, low = split(basis / ff)
        for d in range(nd):
            h = h_ref[i, :, lax.rem(meta_ref[1] + d, nd)]
            h = h.reshape(-1, h.shape[-1])
            zs[d][i] = (dot(h, hi, NT) + dot(h, low, NT)).T


def own_kernel(meta_ref, basis_ref, left_ref, r_ref, out_ref, mom_ref):
    count, rank, ff = basis_ref.shape
    local = out_ref.shape[-1]
    y = meta_ref[3]
    for i in range(count):
        b = basis_ref[i]
        own = b[:, :local]
        for a in range(1, ff // local):
            own = jnp.where(y == a, b[:, a * local : (a + 1) * local], own)
        out_ref[i] = own
        inner = dot(b, left_ref[i], NT, HIGHEST) * (MOMENTUM_DECAY / ff)
        mom_ref[i] = dot(inner, r_ref[i], NN, HIGHEST)


def coefficient_kernel(counts, skipped, nd, unread, *refs):
    nb = sum(counts)
    pieces, refs = refs[:nb], refs[nb:]
    zs, refs = refs[:nd], refs[nd:]
    poss, refs = refs[: len(counts)], refs[len(counts) + unread :]
    outs, w_scr = refs[:nd], refs[nd]
    local, rank, slots = zs[0].shape
    count = nd * local
    every = poss[0].shape[0] // (2 * counts[0])
    tokens = poss[0].shape[1]
    rows = count * rank
    width = outs[0].shape[-1]
    place = lax.broadcasted_iota(jnp.int32, (slots, nb * tokens), 0).astype(F32).astype(BF)
    for q in range(count):
        line = lambda gate: jnp.concatenate(
            [
                r[(gate * n + b) * every + skipped + q : (gate * n + b) * every + skipped + q + 1]
                for r, n in zip(poss, counts)
                for b in range(n)
            ],
            axis=1,
        )
        w = folded(dot(stacked(zs[q // local][q % local]), one_hot(place, line(0)))) * line(1)
        hi, low = split(w)
        w_scr[q * rank : (q + 1) * rank] = hi
        w_scr[rows + q * rank : rows + (q + 1) * rank] = low
    step = 256

    @pl.loop(0, width // step)
    def _(n):
        cols = pl.ds(pl.multiple_of(n * step, step), step)
        x = jnp.concatenate([ref[:, cols] for ref in pieces], axis=0)
        total = folded(dot(w_scr[...], x))
        for q in range(count):
            ref = outs[q // local]
            ref[q % local, :, cols] = total[q * rank : (q + 1) * rank].astype(ref.dtype)


def body(cotangent, gates, expert_ids, hidden, momentum_left, momentum_right, sketch):
    nx, nc = NX, NC
    ne, ny = lax.axis_size("expert"), lax.axis_size("zero")
    nz = ne // (nx * nc)
    local, _, ff = hidden.shape
    tokens, width = cotangent.shape
    rank = sketch.shape[2]
    me, y = lax.axis_index("expert"), lax.axis_index("zero")
    z, x, c = me // (nx * nc), me // nc % nx, me % nc
    meta = jnp.stack([z, x, c, y]).astype(jnp.int32)

    def shift(v, dz=0, dx=0, dc=0):
        pairs = []
        for e in range(ne):
            a, b, k = e // (nx * nc), e // nc % nx, e % nc
            to = ((a + dz) % nz * nx + (b + dx) % nx) * nc + (k + dc) % nc
            pairs.append((e, to))
        return lax.ppermute(v, "expert", pairs)

    def shift_y(v, dy):
        return lax.ppermute(v, "zero", [(a, (a + dy) % ny) for a in range(ny)])

    def shaped(s, t=F32):
        return jax.ShapeDtypeStruct(s, t)

    mine = call(
        pack_kernel,
        shaped((tokens, width + tokens), BF),
        (cotangent, gates.T, expert_ids.T),
        specs=[ANY] * 3,
        limit=58 << 20,
        scratch=[
            pltpu.VMEM((gates.shape[1], tokens), F32),
            pltpu.VMEM((gates.shape[1], tokens), jnp.int32),
            pltpu.VMEM((tokens, tokens), BF),
            pltpu.SemaphoreType.DMA((4,)),
        ],
    )

    st = jnp.swapaxes(sketch, 1, 2)
    rows = local * rank
    two = call(sketch_kernel, shaped((2, rows, width), BF), (st.reshape(rows, width),))
    lt = jnp.swapaxes(momentum_left, 1, 2)
    slots = nz * nc * CAP
    count = nx * local
    half = nz // 2

    def along(v, axis="z"):
        pairs = []
        for e in range(ne):
            a, b, k = e // (nx * nc), e // nc % nx, e % nc
            if axis == "z":
                pairs.append((e, ((a + 1 - 2 * k) % nz * nx + b) * nc + k))
            else:
                pairs.append((e, (a * nx + (b - 1 + 2 * k) % nx) * nc + k))
        return lax.ppermute(v, "expert", pairs)

    def swap(v):
        return shift(v, dc=1)

    def project(named, sketches, earlier, parts=1):
        places, blocks = zip(*named)
        nb = len(blocks)
        whole = len(sketches) == 1
        outs = [shaped((count // parts, rank, slots))] * parts
        products = call(
            functools.partial(project_kernel, places, nz, nx, len(earlier), whole),
            outs
            + ([] if whole else [shaped((2 * count * rank, width), BF)])
            + [shaped((2 * nb * count, tokens))],
            (meta, *blocks, *sketches, *earlier),
            specs=[SMEM] + [VMEM] * (nb + len(sketches) + len(earlier)),
            scratch=[pltpu.VMEM((count * rank, nb * tokens), F32)],
            flops=2 * 2 * count * rank * nb * tokens * width,
        )
        return nb, blocks, products[:parts], products[-1], products[-2]

    def ring(k, p, q):
        return [((k, 1), p), ((k, 0), q), ((-k, 0), swap(p)), ((-k, 1), swap(q))]

    lefts = [lt] + [shift_y(lt, d) for d in range(1, ny)]
    left_full, mom = call(
        momentum_kernel,
        [shaped((local, rank, ff))] * 2,
        (meta, st, momentum_right, *lefts),
        specs=[SMEM] + [VMEM] * (2 + ny),
        scratch=[pltpu.VMEM((ny, local, rank, ff // ny), F32)],
    )
    p = along(mine)
    sibling = swap(mine)
    q = along(sibling)
    [p], [q] = after([p], lefts[1]), after([q], lefts[2])
    near = [shift(two, dx=-1), shift(two, dx=1)]
    first = [((0, 1), mine), ((0, 0), sibling)] + ring(1, p, q)
    farther, token = call(
        forward_kernel,
        [shaped((2, rows, width), BF), shaped((8, 128))],
        (meta, *near),
        specs=[SMEM, VMEM, VMEM],
    )
    far = along(farther, "x")
    p, [q] = along(p), after([along(q)], token, *lefts[3:])
    second = ring(2, p, q)
    a = project(first, [two, near[0], far, near[1]], [])
    all_s = [a[4]]
    p, q = along(p), along(q)
    third = ring(3, p, q)
    b = project(second, all_s, a[2])
    [p] = after([along(p)], b[3], mom)
    fourth = [((4, 1), p), ((4, 0), swap(p))]
    e = project(third, all_s, b[2])
    f = project(fourth, all_s, e[2], nx)
    steps = [a, b, e, f]
    counts = [v[0] for v in steps]
    pieces = [block for v in steps for block in v[1]]
    products = [f[2][0]] + [shift(f[2][d], dx=d) for d in range(1, nx)]

    h = hidden.reshape(local, nz, nx, nc * CAP, ff)
    part = call(
        functools.partial(sum_kernel, nx),
        shaped((local, rank, ff), BF),
        (meta, *products, h, mom),
        specs=[SMEM] + [VMEM] * (nx + 2),
        limit=NARROW,
    )
    parts = [part] + [shift_y(part, d) for d in range(1, ny)]
    basis, *coded = call(
        functools.partial(basis_kernel, ny, nx),
        [shaped((local, rank, ff))] + [shaped((local, rank, slots))] * nx,
        (meta, *parts, h),
        specs=[SMEM] + [VMEM] * (ny + 1),
        limit=NARROW,
    )
    coded = [coded[0]] + [shift(coded[d], dx=d) for d in range(1, nx)]
    coded = [coded[-d % nx] for d in range(nx)]
    own_basis, own_mom = call(
        own_kernel,
        [shaped((local, rank, ff // ny)), shaped(momentum_right.shape)],
        (meta, basis, left_full, momentum_right),
        specs=[SMEM] + [VMEM] * 3,
        limit=NARROW,
    )
    def coefficients(groups, *unread):
        return call(
            functools.partial(
                coefficient_kernel, counts, groups[0] * local, len(groups), len(unread)
            ),
            [shaped((local, rank, width), BF if d else F32) for d in groups],
            (*pieces, *[coded[d] for d in groups], *[v[3] for v in steps], *unread),
            scratch=[pltpu.VMEM((2 * len(groups) * local * rank, sum(counts) * tokens), BF)],
            flops=2 * 2 * len(groups) * local * rank * sum(counts) * tokens * width,
        )

    coeff = coefficients(list(range(nx)), own_mom)
    total = coeff[0]
    for d in range(1, nx):
        total = total + shift(coeff[d], dx=d).astype(F32)
    cols = width // ny

    def columns(d):
        return lax.dynamic_slice_in_dim(total, lax.rem(y + d, ny) * cols, cols, axis=2)

    out = columns(0) + own_mom
    for d in range(1, ny):
        out = out + shift_y(columns(d), d)
    return jnp.swapaxes(own_basis, 1, 2), out


def solution(mesh):
    return jax.shard_map(
        body,
        mesh=mesh,
        in_specs=(
            P(("expert", "zero"), None),
            P(("expert", "zero"), None),
            P(("expert", "zero"), None),
            P("expert", "zero", None),
            P("expert", "zero", None),
            P("expert", None, "zero"),
            P("expert", None, None),
        ),
        out_specs=(P("expert", "zero", None), P("expert", None, "zero")),
        check_vma=False,
    )
```

```python
import functools

import jax
import jax.numpy as jnp
from jax import lax
from jax.experimental import pallas as pl
from jax.experimental.pallas import tpu as pltpu
from jax.sharding import PartitionSpec as P

NX, NC = 4, 2
CAP = 16
MOMENTUM_DECAY = 0.9

WIDE, NARROW = 20 << 20, 8 << 20

BF, F32 = jnp.bfloat16, jnp.float32
HIGHEST = lax.Precision.HIGHEST
VMEM = pl.BlockSpec(memory_space=pltpu.VMEM)
ANY = pl.BlockSpec(memory_space=pl.ANY)
HBM = pl.BlockSpec(memory_space=pltpu.HBM)
SMEM = pl.BlockSpec(memory_space=pltpu.SMEM)
NT = (((1,), (1,)), ((), ()))
NN = (((1,), (0,)), ((), ()))


def dot(a, b, dims=NN, precision=None):
    return lax.dot_general(a, b, dims, precision=precision, preferred_element_type=F32)


def split(v):
    hi = v.astype(BF)
    return hi, (v - hi.astype(F32)).astype(BF)


def stacked(v):
    return jnp.concatenate(split(v), axis=0)


def folded(v):
    half = v.shape[0] // 2
    return v[:half] + v[half:]


def call(kernel, outs, args, specs=None, scratch=(), limit=WIDE, flops=0, spaces=None):
    return pl.pallas_call(
        kernel,
        out_shape=outs,
        in_specs=specs or [VMEM] * len(args),
        out_specs=spaces or jax.tree.map(lambda _: VMEM, outs),
        scratch_shapes=list(scratch),
        compiler_params=pltpu.CompilerParams(vmem_limit_bytes=limit),
        cost_estimate=pl.CostEstimate(flops=flops, bytes_accessed=flops // 500, transcendentals=0),
    )(*args)


def after(values, *needs):
    def kernel(*refs):
        for n in range(len(values)):
            refs[len(values) + len(needs) + n][...] = refs[n][...]

    outs = [jax.ShapeDtypeStruct(v.shape, v.dtype) for v in values]
    return call(kernel, outs, (*values, *needs), limit=NARROW)


def pack_kernel(cot_ref, gates_ref, ids_ref, out_ref, g_scr, i_scr, e_scr, sems):
    tokens, width = cot_ref.shape
    main = pltpu.make_async_copy(cot_ref, out_ref.at[:, 0:width], sems.at[0])
    first = pltpu.make_async_copy(gates_ref, g_scr, sems.at[1])
    second = pltpu.make_async_copy(ids_ref, i_scr, sems.at[2])
    main.start()
    first.start()
    second.start()
    first.wait()
    second.wait()
    g = g_scr[...]
    hi = g.astype(BF).astype(F32)
    mid = (g - hi).astype(BF).astype(F32)
    low = g - hi - mid
    ids = i_scr[...].astype(F32)
    rest = jnp.zeros((tokens - 4 * g.shape[0], tokens), F32)
    e_scr[...] = jnp.concatenate([ids, hi, mid, low, rest], axis=0).astype(BF)
    last = pltpu.make_async_copy(e_scr, out_ref.at[:, width : width + tokens], sems.at[3])
    last.start()
    main.wait()
    last.wait()


def sketch_kernel(st_ref, out_ref):
    hi, low = split(st_ref[...])
    out_ref[0] = hi
    out_ref[1] = low


def momentum_kernel(meta_ref, st_ref, r_ref, *refs):
    lefts, (full_ref, mom_ref, rows) = refs[:-3], refs[-3:]
    ny, y = len(lefts), meta_ref[3]
    for d in range(ny):
        rows[lax.rem(y - d + ny, ny)] = lefts[d][...]
    local = lefts[0].shape[-1]
    cols = r_ref.shape[-1]
    for i in range(r_ref.shape[0]):
        part = st_ref[i, :, pl.ds(pl.multiple_of(y * cols, 128), cols)]
        inner = dot(part, r_ref[i], NT, HIGHEST) * MOMENTUM_DECAY
        for a in range(ny):
            block = rows[a, i]
            full_ref[i, :, a * local : (a + 1) * local] = block
            mom_ref[i, :, a * local : (a + 1) * local] = dot(inner, block, NN, HIGHEST)


def forward_kernel(meta_ref, right_ref, left_ref, out_ref, token_ref):
    out_ref[...] = jnp.where(meta_ref[2] == 0, right_ref[...], left_ref[...])
    token_ref[...] = jnp.zeros_like(token_ref)


def one_hot(place, line):
    return jnp.where(place == line.astype(BF), jnp.ones((), BF), jnp.zeros((), BF))


def project_kernel(places, nz, ng, carried, whole, meta_ref, *refs):
    nb = len(places)
    pieces, refs = refs[:nb], refs[nb:]
    fed = 1 if whole else ng
    sketches, earlier, refs = refs[:fed], refs[fed : fed + carried], refs[fed + carried :]
    outs, (pos_ref, y_scr) = refs[:-2], refs[-2:]
    all_s = sketches[0] if whole else outs[-1]
    outs = outs if whole else outs[:-1]
    _, rank, slots = outs[0].shape
    count = len(outs) * outs[0].shape[0]
    local = count // ng
    rows = count * rank
    gates = nb * count
    tokens = pieces[0].shape[0]
    width = all_s.shape[1]
    if not whole:
        per = rows // ng
        for d in range(ng):
            for k in range(2):
                at = k * rows + d * per
                all_s[at : at + per] = sketches[d][k]
    which = lax.broadcasted_iota(jnp.int32, (count, tokens), 0)
    before = (
        lax.broadcasted_iota(jnp.int32, (tokens, tokens), 0)
        < lax.broadcasted_iota(jnp.int32, (tokens, tokens), 1)
    ).astype(F32).astype(BF)
    z, x, c = meta_ref[0], meta_ref[1], meta_ref[2]
    experts = [
        (((z * NX + lax.rem(x + q // local, ng)) * NC + c) * local + q % local).astype(F32)
        for q in range(count)
    ]
    named, weights = [], []
    for b in range(nb):
        extra = pieces[b][0:32, width:].astype(F32)
        ids = extra[0:8]
        g = extra[8:16] + extra[16:24] + extra[24:32]
        member = jnp.zeros((count, tokens), F32)
        gate = jnp.zeros((count, tokens), F32)
        for q in range(count):
            hit = ids == experts[q]
            m = jnp.sum(jnp.where(hit, 1.0, 0.0), axis=0, keepdims=True)
            w = jnp.sum(jnp.where(hit, g, 0.0), axis=0, keepdims=True)
            member = jnp.where(which == q, m, member)
            gate = jnp.where(which == q, w, gate)
        named.append(member)
        weights.append(gate)
    member = jnp.concatenate(named, axis=0)
    slot = dot(member.astype(BF), before)
    for b, (k, same) in enumerate(places):
        here = slice(b * count, (b + 1) * count)
        source = c if same else NC - 1 - c
        base = ((lax.rem(z - (1 - 2 * c) * k + nz, nz) * NC + source) * CAP).astype(F32)
        pos_ref[here] = jnp.where(member[here] > 0.5, slot[here] + base, -1.0)
        pos_ref[gates + b * count : gates + (b + 1) * count] = weights[b]
    for b in range(0, nb, 2):
        pair = slice(b * tokens, (b + 2) * tokens)
        x2 = jnp.concatenate([ref[:, :width] for ref in pieces[b : b + 2]], axis=0)
        y_scr[:, pair] = folded(dot(all_s[...], x2, NT))
    place = lax.broadcasted_iota(jnp.int32, (slots, nb * tokens), 0).astype(F32).astype(BF)
    for q in range(count):
        line = lambda at: jnp.concatenate(
            [pos_ref[at + b * count + q : at + b * count + q + 1] for b in range(nb)], axis=1
        )
        v = y_scr[q * rank : (q + 1) * rank] * line(gates)
        r = folded(dot(stacked(v), one_hot(place, line(0)), NT))
        per = count // len(outs)
        outs[q // per][q % per] = r + earlier[0][q] if carried else r


def sum_kernel(nd, meta_ref, *refs):
    parts, (h_ref, mom_ref, out_ref) = refs[:nd], refs[nd:]
    for i in range(out_ref.shape[0]):
        total = mom_ref[i]
        for d in range(nd):
            h = h_ref[i, :, lax.rem(meta_ref[1] - d + nd, nd)]
            h = h.reshape(-1, h.shape[-1])
            total = total + folded(dot(stacked(parts[d][i]), h))
        out_ref[i] = total.astype(out_ref.dtype)


def basis_kernel(ny, nd, meta_ref, *refs):
    parts, (h_ref, basis_ref), zs = refs[:ny], refs[ny : ny + 2], refs[ny + 2 :]
    count, rank, ff = basis_ref.shape
    row = lax.broadcasted_iota(jnp.int32, (rank, 2 * rank), 0)
    lane = lax.broadcasted_iota(jnp.int32, (rank, 2 * rank), 1)
    sk, work = [], []
    for i in range(count):
        s = parts[0][i].astype(F32)
        for d in range(1, ny):
            s = s + parts[d][i].astype(F32)
        sk.append(s)
        both = jnp.concatenate([jnp.zeros_like(s), s], axis=0)
        a = dot(s, both, NT, HIGHEST) / ff
        work.append(jnp.where(lane == row, 1.0, a))
    for j in range(rank):
        for i in range(count):
            a = work[i]
            line = a[j : j + 1]
            pivot = jnp.broadcast_to(line[:, rank + j : rank + j + 1], line.shape)
            column = jnp.broadcast_to(a[:, rank + j : rank + j + 1], a.shape)
            work[i] = a - jnp.where(row > j, column, 0.0) * (line / pivot)
    for i in range(count):
        diag = jnp.sum(jnp.where(lane == row + rank, work[i], 0.0), axis=1, keepdims=True)
        inverse = (work[i] / jnp.sqrt(diag))[:, :rank]
        basis = dot(inverse, sk[i], NN, HIGHEST)
        basis_ref[i] = basis
        b = stacked(basis / ff)
        for d in range(nd):
            h = h_ref[i, :, lax.rem(meta_ref[1] + d, nd)]
            h = h.reshape(-1, h.shape[-1])
            zs[d][i] = folded(dot(b, h, NT))


def own_kernel(meta_ref, basis_ref, left_ref, r_ref, out_ref, mom_ref):
    count, rank, ff = basis_ref.shape
    local = out_ref.shape[-1]
    y = meta_ref[3]
    for i in range(count):
        b = basis_ref[i]
        own = b[:, :local]
        for a in range(1, ff // local):
            own = jnp.where(y == a, b[:, a * local : (a + 1) * local], own)
        out_ref[i] = own
        inner = dot(b, left_ref[i], NT, HIGHEST) * (MOMENTUM_DECAY / ff)
        mom_ref[i] = dot(inner, r_ref[i], NN, HIGHEST)


def coefficient_kernel(counts, skipped, nd, unread, *refs):
    nb = sum(counts)
    pieces, refs = refs[:nb], refs[nb:]
    zs, refs = refs[:nd], refs[nd:]
    poss, refs = refs[: len(counts)], refs[len(counts) + unread :]
    outs, w_scr = refs[:nd], refs[nd]
    local, rank, slots = zs[0].shape
    count = nd * local
    every = poss[0].shape[0] // (2 * counts[0])
    tokens = poss[0].shape[1]
    rows = count * rank
    width = outs[0].shape[-1]
    place = lax.broadcasted_iota(jnp.int32, (slots, nb * tokens), 0).astype(F32).astype(BF)
    for q in range(count):
        line = lambda gate: jnp.concatenate(
            [
                r[(gate * n + b) * every + skipped + q : (gate * n + b) * every + skipped + q + 1]
                for r, n in zip(poss, counts)
                for b in range(n)
            ],
            axis=1,
        )
        w = folded(dot(stacked(zs[q // local][q % local]), one_hot(place, line(0)))) * line(1)
        hi, low = split(w)
        w_scr[q * rank : (q + 1) * rank] = hi
        w_scr[rows + q * rank : rows + (q + 1) * rank] = low
    step = 256

    @pl.loop(0, width // step)
    def _(n):
        cols = pl.ds(pl.multiple_of(n * step, step), step)
        x = jnp.concatenate([ref[:, cols] for ref in pieces], axis=0)
        total = folded(dot(w_scr[...], x))
        for q in range(count):
            ref = outs[q // local]
            ref[q % local, :, cols] = total[q * rank : (q + 1) * rank].astype(ref.dtype)


def body(cotangent, gates, expert_ids, hidden, momentum_left, momentum_right, sketch):
    nx, nc = NX, NC
    ne, ny = lax.axis_size("expert"), lax.axis_size("zero")
    nz = ne // (nx * nc)
    local, _, ff = hidden.shape
    tokens, width = cotangent.shape
    rank = sketch.shape[2]
    me, y = lax.axis_index("expert"), lax.axis_index("zero")
    z, x, c = me // (nx * nc), me // nc % nx, me % nc
    meta = jnp.stack([z, x, c, y]).astype(jnp.int32)

    def shift(v, dz=0, dx=0, dc=0):
        pairs = []
        for e in range(ne):
            a, b, k = e // (nx * nc), e // nc % nx, e % nc
            to = ((a + dz) % nz * nx + (b + dx) % nx) * nc + (k + dc) % nc
            pairs.append((e, to))
        return lax.ppermute(v, "expert", pairs)

    def shift_y(v, dy):
        return lax.ppermute(v, "zero", [(a, (a + dy) % ny) for a in range(ny)])

    def shaped(s, t=F32):
        return jax.ShapeDtypeStruct(s, t)

    mine = call(
        pack_kernel,
        shaped((tokens, width + tokens), BF),
        (cotangent, gates.T, expert_ids.T),
        specs=[ANY] * 3,
        limit=58 << 20,
        scratch=[
            pltpu.VMEM((gates.shape[1], tokens), F32),
            pltpu.VMEM((gates.shape[1], tokens), jnp.int32),
            pltpu.VMEM((tokens, tokens), BF),
            pltpu.SemaphoreType.DMA((4,)),
        ],
    )

    st = jnp.swapaxes(sketch, 1, 2)
    rows = local * rank
    two = call(sketch_kernel, shaped((2, rows, width), BF), (st.reshape(rows, width),))
    lt = jnp.swapaxes(momentum_left, 1, 2)
    slots = nz * nc * CAP
    count = nx * local
    half = nz // 2

    def along(v, axis="z"):
        pairs = []
        for e in range(ne):
            a, b, k = e // (nx * nc), e // nc % nx, e % nc
            if axis == "z":
                pairs.append((e, ((a + 1 - 2 * k) % nz * nx + b) * nc + k))
            else:
                pairs.append((e, (a * nx + (b - 1 + 2 * k) % nx) * nc + k))
        return lax.ppermute(v, "expert", pairs)

    def swap(v):
        return shift(v, dc=1)

    def project(named, sketches, earlier, parts=1):
        places, blocks = zip(*named)
        nb = len(blocks)
        whole = len(sketches) == 1
        outs = [shaped((count // parts, rank, slots))] * parts
        products = call(
            functools.partial(project_kernel, places, nz, nx, len(earlier), whole),
            outs
            + ([] if whole else [shaped((2 * count * rank, width), BF)])
            + [shaped((2 * nb * count, tokens))],
            (meta, *blocks, *sketches, *earlier),
            specs=[SMEM] + [VMEM] * (nb + len(sketches) + len(earlier)),
            scratch=[pltpu.VMEM((count * rank, nb * tokens), F32)],
            flops=2 * 2 * count * rank * nb * tokens * width,
        )
        return nb, blocks, products[:parts], products[-1], products[-2]

    def ring(k, p, q):
        return [((k, 1), p), ((k, 0), q), ((-k, 0), swap(p)), ((-k, 1), swap(q))]

    lefts = [lt] + [shift_y(lt, d) for d in range(1, ny)]
    left_full, mom = call(
        momentum_kernel,
        [shaped((local, rank, ff))] * 2,
        (meta, st, momentum_right, *lefts),
        specs=[SMEM] + [VMEM] * (2 + ny),
        scratch=[pltpu.VMEM((ny, local, rank, ff // ny), F32)],
    )
    p = along(mine)
    sibling = swap(mine)
    q = along(sibling)
    [p], [q] = after([p], lefts[1]), after([q], lefts[2])
    near = [shift(two, dx=-1), shift(two, dx=1)]
    first = [((0, 1), mine), ((0, 0), sibling)] + ring(1, p, q)
    farther, token = call(
        forward_kernel,
        [shaped((2, rows, width), BF), shaped((8, 128))],
        (meta, *near),
        specs=[SMEM, VMEM, VMEM],
    )
    far = along(farther, "x")
    p, [q] = along(p), after([along(q)], token, *lefts[3:])
    second = ring(2, p, q)
    a = project(first, [two, near[0], far, near[1]], [])
    all_s = [a[4]]
    p, q = along(p), along(q)
    third = ring(3, p, q)
    b = project(second, all_s, a[2])
    [p] = after([along(p)], b[3], mom)
    fourth = [((4, 1), p), ((4, 0), swap(p))]
    e = project(third, all_s, b[2])
    f = project(fourth, all_s, e[2], nx)
    steps = [a, b, e, f]
    counts = [v[0] for v in steps]
    pieces = [block for v in steps for block in v[1]]
    products = [f[2][0]] + [shift(f[2][d], dx=d) for d in range(1, nx)]

    h = hidden.reshape(local, nz, nx, nc * CAP, ff)
    part = call(
        functools.partial(sum_kernel, nx),
        shaped((local, rank, ff), BF),
        (meta, *products, h, mom),
        specs=[SMEM] + [VMEM] * (nx + 2),
        limit=NARROW,
    )
    parts = [part] + [shift_y(part, d) for d in range(1, ny)]
    basis, *coded = call(
        functools.partial(basis_kernel, ny, nx),
        [shaped((local, rank, ff))] + [shaped((local, rank, slots))] * nx,
        (meta, *parts, h),
        specs=[SMEM] + [VMEM] * (ny + 1),
        limit=NARROW,
    )
    coded = [coded[0]] + [shift(coded[d], dx=d) for d in range(1, nx)]
    coded = [coded[-d % nx] for d in range(nx)]
    own_basis, own_mom = call(
        own_kernel,
        [shaped((local, rank, ff // ny)), shaped(momentum_right.shape)],
        (meta, basis, left_full, momentum_right),
        specs=[SMEM] + [VMEM] * 3,
        limit=NARROW,
    )
    def coefficients(groups, *unread):
        return call(
            functools.partial(
                coefficient_kernel, counts, groups[0] * local, len(groups), len(unread)
            ),
            [shaped((local, rank, width), BF if d else F32) for d in groups],
            (*pieces, *[coded[d] for d in groups], *[v[3] for v in steps], *unread),
            scratch=[pltpu.VMEM((2 * len(groups) * local * rank, sum(counts) * tokens), BF)],
            flops=2 * 2 * len(groups) * local * rank * sum(counts) * tokens * width,
        )

    coeff = coefficients(list(range(nx)), own_mom)
    total = coeff[0]
    for d in range(1, nx):
        total = total + shift(coeff[d], dx=d).astype(F32)
    cols = width // ny

    def columns(d):
        return lax.dynamic_slice_in_dim(total, lax.rem(y + d, ny) * cols, cols, axis=2)

    out = columns(0) + own_mom
    for d in range(1, ny):
        out = out + shift_y(columns(d).astype(BF), d).astype(F32)
    return jnp.swapaxes(own_basis, 1, 2), out


def solution(mesh):
    return jax.shard_map(
        body,
        mesh=mesh,
        in_specs=(
            P(("expert", "zero"), None),
            P(("expert", "zero"), None),
            P(("expert", "zero"), None),
            P("expert", "zero", None),
            P("expert", "zero", None),
            P("expert", None, "zero"),
            P("expert", None, None),
        ),
        out_specs=(P("expert", "zero", None), P("expert", None, "zero")),
        check_vma=False,
    )
```
